32 devices in a mesh: animal: 8 (over y, x, core), marker: 4 (over z).
Axes of the slice: x: 2, y: 2, z: 4, core: 2. Of those that a mesh axis runs over, the one named last changes fastest.
Arguments:
- genotypes: bfloat16 [24576, 25600], P('animal', 'marker'), may hold values from -4 to 4
- direction: bfloat16 [25600, 256], P('marker'), may hold values from -6 to 6
- ridge: float32 [25600], P('marker'), may hold values from 0.5 to 2
- send_list: int32 [8, 8, 2], P('animal'), may hold values from 0 to 23, as said below
- rel_index: int32 [192, 4], P('animal'), may hold values from 0 to 39, as said below
- rel_count: int32 [192], P('animal'), may hold values from 1 to 4, as said below
- rel_prec: bfloat16 [192, 4, 128, 128], P('animal'), may hold values from -0.375 to 0.375
Outputs:
- gradient: float32 [25600, 256], P(('marker', 'animal'))
The draws below stay inside these ranges and needn't reach their ends.
Inputs may be any that keep to these rules, and one draw needn't show every extreme that they name: `send_list`: every entry names one of the sender's own 24 blocks. `rel_index`: entry j of block g indexes g's device's source table; entry 0 is g's own block, g % 24. `rel_count`: the first block of every device has 4 live slots.
All inputs are finite; a program needn't handle non-finite values.
Results may differ from the reference program's by a relative error of at most 0.0033.
Values may be sent and summed in bfloat16 or wider, within the bound.
No kernel may reach another device: no remote copies, remote signals or barrier semaphores. Data moves between devices by JAX's collectives and lax.ppermute only.
A program may use at most 128 MiB of HBM per device.

```python
import math
import jax
import jax.numpy as jnp
from jax import lax

MARKERS = 25600
K = 256
BLK = 128
NREL = 4
SLOTS = 2
ANIMALS = 24576
BLOCKS = 192
BLK_DEV = 24


def draw_send_list(key, part):
    peers = BLOCKS // BLK_DEV
    listed = jax.random.randint(jax.random.fold_in(key, 11), (peers, peers, SLOTS), 0, BLK_DEV, dtype=jnp.int32)
    listed = listed.at[:, 0, 0].set(BLK_DEV - 1)
    return listed.at[:, peers - 1, 0].set(0)


def draw_rel_index(key, part):
    peers = BLOCKS // BLK_DEV
    reach = BLK_DEV + peers * SLOTS
    chosen = jax.random.randint(jax.random.fold_in(key, 12), (BLOCKS, NREL), 0, reach, dtype=jnp.int32)
    own_block = jnp.arange(BLOCKS, dtype=jnp.int32) % BLK_DEV
    chosen = chosen.at[:, 0].set(own_block)
    return chosen.at[0, NREL - 1].set(reach - 1)


def draw_rel_count(key, part):
    peers = BLOCKS // BLK_DEV
    heavy = jax.random.randint(jax.random.fold_in(key, 13), (peers,), 0, 2, dtype=jnp.int32)
    even_law = jax.random.randint(jax.random.fold_in(key, 14), (BLOCKS,), 1, NREL + 1, dtype=jnp.int32)
    first_low = jax.random.randint(jax.random.fold_in(key, 15), (BLOCKS,), 0, NREL, dtype=jnp.int32)
    second_low = jax.random.randint(jax.random.fold_in(key, 16), (BLOCKS,), 0, NREL, dtype=jnp.int32)
    low_law = 1 + jnp.minimum(first_low, second_low)
    heavy_block = jnp.repeat(heavy, BLK_DEV)
    counts = jnp.where(heavy_block == 1, even_law, low_law).astype(jnp.int32)
    counts = counts.at[::BLK_DEV].set(NREL)
    return counts.at[BLK_DEV - 1].set(1)


def strengthened(array, rng, source, target, blocks, factor):
    def block_of(dim):
        return (jnp.arange(array.shape[dim]) // (array.shape[dim] // blocks)).reshape((-1,) + (1,) * (array.ndim - 1 - dim))

    near = jax.random.permutation(rng, blocks)[block_of(target)]
    other_side = (block_of(target) + blocks // 2) % blocks
    return jnp.where((block_of(source) == near) | (block_of(source) == other_side), factor * array, array)


def block_scale(own_key, shape, pieces, least, high):
    def one(dim, blocks):
        heights = jax.random.uniform(jax.random.fold_in(jax.random.fold_in(own_key, 6), dim), (blocks,), jnp.float32, least / len(pieces), high / len(pieces))
        return jnp.repeat(jnp.exp(heights), shape[dim] // blocks).reshape((-1,) + (1,) * (len(shape) - dim - 1))

    gain = one(*pieces[0])
    for cut in pieces[1:]:
        gain = gain * one(*cut)
    return gain


def bell_draw(stream_key, extent, scale, limit, pieces=(), kind=jnp.bfloat16):
    entries = jax.random.normal(stream_key, extent, jnp.float32) * scale
    if len(pieces) > 0:
        entries = block_scale(stream_key, extent, pieces, -0.22, 0.18) * entries
    return jnp.clip(entries, min=-limit, max=limit).astype(kind)


def heavy_noise(stream_key, extent, scale, most, pieces, heavy, kind=jnp.bfloat16):
    drawn = scale * jax.random.normal(stream_key, extent, jnp.float32)
    if pieces:
        drawn = drawn * block_scale(stream_key, extent, pieces, -0.22, 0.18)
    return jnp.clip(strengthened(drawn, jax.random.fold_in(stream_key, 3), *heavy), -most, most).astype(kind)


def setup_inputs(seed: int = 0) -> dict:
    splits = jax.random.split(jax.random.key(seed), 8)
    genotypes = heavy_noise(splits[0], (ANIMALS, MARKERS), 1.0, 4.0, ((0, 8), (1, 4)), (0, 1, 8, 2.0))
    direction = bell_draw(splits[1], (MARKERS, K), 1.0, 6.0, ((0, 4),))
    ridge = jnp.clip(jnp.exp(math.log(2.0) - 1.3862944 * jax.random.uniform(splits[2], (MARKERS,), jnp.float32) ** block_scale(splits[2], (MARKERS,), ((0, 4),), -0.2, 0.2)), 0.5, 2.0)
    send_list = draw_send_list(jax.random.fold_in(splits[7], 71), 0)
    rel_index = draw_rel_index(jax.random.fold_in(splits[7], 71), 0)
    rel_count = draw_rel_count(jax.random.fold_in(splits[7], 71), 0)
    rel_prec = bell_draw(splits[6], (BLOCKS, NREL, BLK, BLK), (2 * BLK) ** -0.5, 0.375, ((0, 8),))
    return dict(genotypes=genotypes, direction=direction, ridge=ridge, send_list=send_list, rel_index=rel_index, rel_count=rel_count, rel_prec=rel_prec)


def reference(genotypes, direction, ridge, send_list, rel_index, rel_count, rel_prec):
    animal_sum = (jnp.dot(genotypes, direction, preferred_element_type=jnp.float32) * (1.0 / math.sqrt(MARKERS))).astype(jnp.bfloat16)
    animal_blocks = animal_sum.reshape(BLOCKS, BLK, K)
    owner_dev = (jnp.arange(BLOCKS, dtype=jnp.int32) // BLK_DEV)[:, None]
    far_index = jnp.maximum(rel_index - BLK_DEV, 0).astype(jnp.int32)
    peer_dev = (far_index // SLOTS).astype(jnp.int32)
    slot_index = (far_index % SLOTS).astype(jnp.int32)
    owner_full = jnp.broadcast_to(owner_dev, rel_index.shape).astype(jnp.int32)
    sent_block = send_list[peer_dev, owner_full, slot_index]
    source_block = jnp.where(rel_index < BLK_DEV, owner_full * BLK_DEV + rel_index, peer_dev * BLK_DEV + sent_block).astype(jnp.int32)
    active = jnp.arange(NREL, dtype=jnp.int32)[None, :] < rel_count[:, None]

    def relative_block(packed):
        precision, chosen, active_row = packed
        gathered = animal_blocks[chosen]
        gathered = jnp.where(active_row[:, None, None], gathered, jnp.zeros_like(gathered))
        return jnp.einsum('jrc,jck->rk', precision.astype(jnp.float32), gathered.astype(jnp.float32)).astype(jnp.bfloat16)
    relative_sum = lax.map(relative_block, (rel_prec, source_block, active)).reshape(ANIMALS, K)
    gradient = jnp.dot(genotypes.T, relative_sum, preferred_element_type=jnp.float32) * (1.0 / math.sqrt(ANIMALS))
    return gradient + ridge[:, None] * direction.astype(jnp.float32)
```

```python
import functools
import math

import jax
import jax.numpy as jnp
from jax import lax
from jax.experimental import pallas as pl
from jax.experimental.pallas import tpu as pltpu
from jax.sharding import PartitionSpec as P

MARKERS = 25600
BLK = 128
VMEM_LIMIT = 48 * 1024 * 1024


def divisor(total, unit, most):
    best = unit
    for size in range(unit, most + 1, unit):
        if total % size == 0:
            best = size
    return best


def forward_kernel(scale, geno_ref, direction_ref, low_ref, high_ref):
    half = low_ref.shape[1]
    product = scale * jnp.dot(
        geno_ref[...], direction_ref[...], preferred_element_type=jnp.float32
    )
    low_ref[...] = product[:, :half]
    high_ref[...] = product[:, half:]


def forward_product(genotypes, direction, scale, first, rows):
    depth, cols = direction.shape
    tile = divisor(rows, BLK, 2 * BLK)
    start = first // tile
    return pl.pallas_call(
        functools.partial(forward_kernel, scale),
        grid=(rows // tile,),
        in_specs=[
            pl.BlockSpec((tile, depth), lambda i: (start + i, 0)),
            pl.BlockSpec((depth, cols), lambda i: (0, 0), pipeline_mode=pl.Buffered(1)),
        ],
        out_specs=[pl.BlockSpec((tile, cols // 2), lambda i: (i, 0))] * 2,
        out_shape=[jax.ShapeDtypeStruct((rows, cols // 2), jnp.float32)] * 2,
        compiler_params=pltpu.CompilerParams(vmem_limit_bytes=VMEM_LIMIT),
        cost_estimate=pl.CostEstimate(
            flops=2 * rows * depth * cols,
            bytes_accessed=2 * (rows + cols) * depth + 4 * rows * cols,
            transcendentals=0,
        ),
        name="forward_product",
    )(genotypes, direction)


def pedigree_kernel(group, own_total, index_ref, count_ref, own_ref, far_ref, prec_ref, out_ref, table):
    step = pl.program_id(0)

    @pl.when(step == 0)
    def _():
        table[:own_total] = own_ref[...]
        table[own_total:] = far_ref[...]

    for b in range(group):
        block = step * group + b
        total = None
        for j in range(prec_ref.shape[1]):
            source = table[index_ref[block, j]]
            source = jnp.where(j < count_ref[block], source, jnp.zeros_like(source))
            term = jnp.dot(prec_ref[b, j], source, preferred_element_type=jnp.float32)
            total = term if total is None else total + term
        out_ref[b] = total.astype(out_ref.dtype)


def pedigree(blocked, incoming, rel_index, rel_count, rel_prec):
    block_total, _, cols = blocked.shape
    far_total = incoming.shape[0]
    slots = rel_prec.shape[1]
    group = divisor(block_total, 1, 6)
    return pl.pallas_call(
        functools.partial(pedigree_kernel, group, block_total),
        grid_spec=pltpu.PrefetchScalarGridSpec(
            num_scalar_prefetch=2,
            grid=(block_total // group,),
            in_specs=[
                pl.BlockSpec((block_total, BLK, cols), lambda i, *_: (0, 0, 0), pipeline_mode=pl.Buffered(1)),
                pl.BlockSpec((far_total, BLK, cols), lambda i, *_: (0, 0, 0), pipeline_mode=pl.Buffered(1)),
                pl.BlockSpec((group, slots, BLK, BLK), lambda i, *_: (i, 0, 0, 0)),
            ],
            out_specs=pl.BlockSpec((group, BLK, cols), lambda i, *_: (i, 0, 0)),
            scratch_shapes=[pltpu.VMEM((block_total + far_total, BLK, cols), jnp.bfloat16)],
        ),
        out_shape=jax.ShapeDtypeStruct(blocked.shape, jnp.bfloat16),
        compiler_params=pltpu.CompilerParams(vmem_limit_bytes=VMEM_LIMIT),
        cost_estimate=pl.CostEstimate(
            flops=2 * block_total * slots * BLK * BLK * cols,
            bytes_accessed=2 * block_total * slots * BLK * BLK + 2 * (2 * block_total + far_total) * BLK * cols,
            transcendentals=0,
        ),
        name="pedigree",
    )(rel_index, rel_count, blocked, incoming, rel_prec)


def backward_kernel(scale, geno_ref, effects_ref, low_ref, high_ref):
    half = low_ref.shape[1]
    product = scale * lax.dot_general(
        geno_ref[...], effects_ref[...], (((0,), (0,)), ((), ())), preferred_element_type=jnp.float32
    )
    low_ref[...] = product[:, :half]
    high_ref[...] = product[:, half:]


def backward_product(genotypes, effects, scale):
    rows, width = genotypes.shape
    cols = effects.shape[1]
    tile = divisor(width, BLK, 5 * BLK)
    return pl.pallas_call(
        functools.partial(backward_kernel, scale),
        grid=(width // tile,),
        in_specs=[
            pl.BlockSpec((rows, tile), lambda i: (0, i)),
            pl.BlockSpec((rows, cols), lambda i: (0, 0), pipeline_mode=pl.Buffered(1)),
        ],
        out_specs=[pl.BlockSpec((tile, cols // 2), lambda i: (i, 0))] * 2,
        out_shape=[jax.ShapeDtypeStruct((width, cols // 2), jnp.float32)] * 2,
        compiler_params=pltpu.CompilerParams(vmem_limit_bytes=VMEM_LIMIT),
        cost_estimate=pl.CostEstimate(
            flops=2 * rows * width * cols,
            bytes_accessed=2 * rows * (width + cols) + 4 * width * cols,
            transcendentals=0,
        ),
        name="backward_product",
    )(genotypes, effects)


def choose(place, options):
    keys = sorted(options)
    value = options[keys[-1]]
    for key in keys[:-1]:
        value = jnp.where(place == key, options[key], value)
    return value


def hop_pairs(devices, parts, step, down):
    links = [k for k in range(devices - 1) if 0 <= step - k < parts]
    if down:
        return [(devices - 1 - k, devices - 2 - k) for k in links]
    return [(k, k + 1) for k in links]


def largest_everywhere(value, devices):
    value = jnp.full((8, 128), value, jnp.float32)
    found = [value]
    for shift in range(1, devices):
        pairs = [(d, (d + shift) % devices) for d in range(devices)]
        found.append(lax.ppermute(value, "marker", pairs))
    return functools.reduce(jnp.maximum, found)[0, 0]


def chain_sums(flows, devices, grow, shrink):
    parts = len(flows[0])
    here = lax.axis_index("marker")
    places = (devices - 1 - here, here)
    arrived = None
    finished = ([], [])
    for step in range(parts + devices - 2):
        sent = []
        for flow, place in enumerate(places):
            ready = {k: flows[flow][step - k] for k in range(devices - 1) if 0 <= step - k < parts}
            payload = choose(place, ready)
            if arrived is not None:
                payload = payload + jnp.where(place == 0, 0.0, arrived[flow].astype(jnp.float32) * shrink)
            sent.append((payload * grow).astype(jnp.float16))
        sent = lax.optimization_barrier(sent)
        arrived = lax.optimization_barrier(
            [
                lax.ppermute(payload, "marker", hop_pairs(devices, parts, step, flow == 0))
                for flow, payload in enumerate(sent)
            ]
        )
        done = step - (devices - 2)
        if done >= 0:
            for flow in range(2):
                finished[flow].append(flows[flow][done] + arrived[flow].astype(jnp.float32) * shrink)
    return finished


def chain_copies(pieces, devices):
    parts = len(pieces)
    here = lax.axis_index("marker")
    places = (here, devices - 1 - here)
    arrived = ([], [])
    for step in range(parts + devices - 2):
        sent = []
        for flow, place in enumerate(places):
            if step == 0:
                payload = pieces[0]
            elif step < parts:
                payload = jnp.where(place == 0, pieces[step], arrived[flow][-1])
            else:
                payload = arrived[flow][-1]
            sent.append(payload)
        sent = lax.optimization_barrier(sent)
        landed = lax.optimization_barrier(
            [
                lax.ppermute(payload, "marker", hop_pairs(devices, parts, step, flow == 1))
                for flow, payload in enumerate(sent)
            ]
        )
        for flow in range(2):
            arrived[flow].append(landed[flow])
    return [
        [
            choose(place, {k: pieces[c] if k == 0 else arrived[flow][c + k - 1] for k in range(devices)})
            for c in range(parts)
        ]
        for flow, place in enumerate(places)
    ]


def halving_sum(blocks, devices, bits):
    levels = devices.bit_length() - 1
    here = lax.axis_index("animal")
    total = blocks.reshape((2,) * levels + blocks.shape[1:])
    left = list(range(levels - 1, -1, -1))
    for bit in bits:
        axis = left.index(bit)
        mine = (here >> bit) & 1
        sent = lax.dynamic_index_in_dim(total, 1 - mine, axis, keepdims=False)
        kept = lax.dynamic_index_in_dim(total, mine, axis, keepdims=False)
        pairs = [(d, d ^ (1 << bit)) for d in range(devices)]
        got = lax.ppermute(sent.astype(jnp.bfloat16), "animal", pairs)
        total = kept + got.astype(jnp.float32)
        left.pop(axis)
    return total


def local(genotypes, direction, ridge, send_list, rel_index, rel_count, rel_prec):
    rows, width = genotypes.shape
    cols = direction.shape[1]
    half = cols // 2
    groups = lax.axis_size("animal")
    devices = lax.axis_size("marker")
    parts = 4
    part_rows = rows // parts
    block_total = rows // BLK

    partial = [
        forward_product(genotypes, direction, 1.0 / math.sqrt(MARKERS), c * part_rows, part_rows)
        for c in range(parts)
    ]
    bound = 4.0 * math.sqrt(MARKERS)
    largest = jnp.max(jnp.abs(direction)).astype(jnp.float32)
    largest = jnp.maximum(largest_everywhere(largest, devices), 1e-30)
    grow = 32768.0 / bound / largest
    shrink = bound / 32768.0 * largest
    low, high = chain_sums([[p[0] for p in partial], [p[1] for p in partial]], devices, grow, shrink)
    first = lax.axis_index("marker") == 0
    own = jnp.concatenate(
        [jnp.where(first, a, b).astype(jnp.bfloat16) for a, b in zip(low, high)], axis=0
    ).reshape(block_total, BLK, half)

    outgoing = own[send_list[0]]
    incoming = lax.all_to_all(outgoing, "animal", split_axis=0, concat_axis=0, tiled=True)
    incoming = incoming.reshape(-1, BLK, half)
    relative = pedigree(own, incoming, rel_index, rel_count, rel_prec).reshape(rows, half)

    pieces = [relative[c * part_rows : (c + 1) * part_rows] for c in range(parts)]
    low, high = chain_copies(pieces, devices)
    effects = jnp.concatenate(
        [jnp.concatenate([a, b], axis=1) for a, b in zip(low, high)], axis=0
    )

    share = width // groups
    low, high = [
        product.reshape(groups, share, half)
        for product in backward_product(genotypes, effects, 1.0 / math.sqrt(groups * rows))
    ]
    levels = list(range(groups.bit_length() - 1))
    gradient = jnp.concatenate(
        [
            halving_sum(low, groups, levels),
            halving_sum(high, groups, levels[:1] + levels[:0:-1]),
        ],
        axis=1,
    )
    start = lax.axis_index("animal") * share
    own_ridge = lax.dynamic_slice_in_dim(ridge, start, share, 0)
    own_direction = lax.dynamic_slice_in_dim(direction, start, share, 0)
    return gradient + own_ridge[:, None] * own_direction.astype(jnp.float32)


def solution(mesh):
    in_specs = (
        P("animal", "marker"),
        P("marker", None),
        P("marker"),
        P("animal", None, None),
        P("animal", None),
        P("animal"),
        P("animal", None, None, None),
    )
    out_specs = P(("marker", "animal"), None)
    return jax.shard_map(local, mesh=mesh, in_specs=in_specs, out_specs=out_specs, check_vma=False)
```

```python
import functools
import math

import jax
import jax.numpy as jnp
from jax import lax
from jax.experimental import pallas as pl
from jax.experimental.pallas import tpu as pltpu
from jax.sharding import PartitionSpec as P

MARKERS = 25600
BLK = 128
MARK = 16
VMEM_LIMIT = 56 * 1024 * 1024


def divisor(total, unit, most):
    best = unit
    for size in range(unit, most + 1, unit):
        if total % size == 0:
            best = size
    return best


def forward_kernel(scale, devices, place_ref, geno_ref, direction_ref, own_ref, *rest):
    sent, turned = rest[:-1], rest[-1]
    blocks, share, _ = own_ref.shape
    product = scale * jnp.dot(geno_ref[...], direction_ref[...], preferred_element_type=jnp.float32)
    largest = jnp.max(jnp.abs(product), axis=(0, 1), keepdims=True)
    power = jnp.clip(jnp.ceil(jnp.log2(largest)), -100.0, 120.0)
    grow = jnp.exp2(14.0 - power)
    turned[...] = product.T
    for shift in range(devices):
        first = pl.multiple_of(lax.rem(place_ref[0] + shift, devices) * share, share)
        for b in range(blocks):
            piece = turned[pl.ds(first, share), b * BLK : (b + 1) * BLK]
            if shift == 0:
                own_ref[b] = piece
            else:
                coded = jnp.round(piece * grow).astype(jnp.int32).astype(jnp.int16)
                sent[shift - 1][b * share : (b + 1) * share] = coded
        if shift > 0:
            mark = jnp.broadcast_to(power, (MARK, BLK)).astype(jnp.int32).astype(jnp.int16)
            sent[shift - 1][blocks * share :] = mark


def forward_product(genotypes, direction, place, devices, scale, first, rows, tile):
    depth, cols = direction.shape
    start = first // tile
    share = cols // devices
    blocks = tile // BLK
    coded = blocks * share + MARK
    steps = rows // tile
    return pl.pallas_call(
        functools.partial(forward_kernel, scale, devices),
        grid_spec=pltpu.PrefetchScalarGridSpec(
            num_scalar_prefetch=1,
            grid=(steps,),
            in_specs=[
                pl.BlockSpec((tile, depth), lambda i, *_: (start + i, 0)),
                pl.BlockSpec((depth, cols), lambda i, *_: (0, 0), pipeline_mode=pl.Buffered(1)),
            ],
            out_specs=[pl.BlockSpec((blocks, share, BLK), lambda i, *_: (i, 0, 0))]
            + [pl.BlockSpec((coded, BLK), lambda i, *_: (i, 0))] * (devices - 1),
            scratch_shapes=[pltpu.VMEM((cols, tile), jnp.float32)],
        ),
        out_shape=[jax.ShapeDtypeStruct((steps * blocks, share, BLK), jnp.float32)]
        + [jax.ShapeDtypeStruct((steps * coded, BLK), jnp.int16)] * (devices - 1),
        compiler_params=pltpu.CompilerParams(vmem_limit_bytes=VMEM_LIMIT),
        cost_estimate=pl.CostEstimate(
            flops=2 * rows * depth * cols,
            bytes_accessed=2 * (rows + cols) * depth + 2 * rows * cols,
            transcendentals=0,
        ),
        name="forward_product",
    )(place, genotypes, direction)


def settle_kernel(parts, blocks, list_ref, *refs):
    owns, coded, (sum_ref, out_ref) = refs[:parts], refs[parts:-2], refs[-2:]
    share = sum_ref.shape[1]
    size = blocks * share + MARK
    at = 0
    for part, own in enumerate(owns):
        for step in range(own.shape[0] // blocks):
            row = step * size
            total = own[step * blocks : (step + 1) * blocks]
            for ref in coded[part::parts]:
                power = ref[row + blocks * share : row + size].astype(jnp.float32)[:1]
                steps = ref[row : row + blocks * share].astype(jnp.float32)
                total = total + (steps * jnp.exp2(power - 14.0)).reshape(blocks, share, BLK)
            sum_ref[at : at + blocks] = total.astype(sum_ref.dtype)
            at += blocks
    for i in range(out_ref.shape[0]):
        out_ref[i] = sum_ref[list_ref[i]]


def settle(owns, coded, send_list, blocks):
    block_total = sum(own.shape[0] for own in owns)
    share = owns[0].shape[1]
    sends = send_list.size
    flat = [ref for one in coded for ref in one]
    return pl.pallas_call(
        functools.partial(settle_kernel, len(owns), blocks),
        grid_spec=pltpu.PrefetchScalarGridSpec(
            num_scalar_prefetch=1,
            grid=(1,),
            in_specs=[pl.BlockSpec(x.shape, lambda i, *_, n=x.ndim: (0,) * n) for x in (*owns, *flat)],
            out_specs=[
                pl.BlockSpec((block_total, share, BLK), lambda i, *_: (0, 0, 0)),
                pl.BlockSpec((sends, share, BLK), lambda i, *_: (0, 0, 0)),
            ],
        ),
        out_shape=[
            jax.ShapeDtypeStruct((block_total, share, BLK), jnp.bfloat16),
            jax.ShapeDtypeStruct((sends, share, BLK), jnp.bfloat16),
        ],
        compiler_params=pltpu.CompilerParams(vmem_limit_bytes=VMEM_LIMIT),
        name="settle",
    )(send_list.reshape(-1), *owns, *flat)


def pedigree_kernel(group, own_total, index_ref, count_ref, own_ref, far_ref, prec_ref, out_ref, table):
    step = pl.program_id(0)

    @pl.when(step == 0)
    def _():
        table[:own_total] = own_ref[...]
        table[own_total:] = far_ref[...]

    for b in range(group):
        block = step * group + b
        total = None
        for j in range(prec_ref.shape[1]):
            source = table[index_ref[block, j]]
            source = jnp.where(j < count_ref[block], source, jnp.zeros_like(source))
            term = lax.dot_general(
                source, prec_ref[b, j], (((1,), (1,)), ((), ())), preferred_element_type=jnp.float32
            )
            total = term if total is None else total + term
        out_ref[b] = total.astype(out_ref.dtype)


def pedigree(blocked, incoming, rel_index, rel_count, rel_prec):
    block_total, share, _ = blocked.shape
    far_total = incoming.shape[0]
    slots = rel_prec.shape[1]
    group = divisor(block_total, 1, 6)
    return pl.pallas_call(
        functools.partial(pedigree_kernel, group, block_total),
        grid_spec=pltpu.PrefetchScalarGridSpec(
            num_scalar_prefetch=2,
            grid=(block_total // group,),
            in_specs=[
                pl.BlockSpec((block_total, share, BLK), lambda i, *_: (0, 0, 0), pipeline_mode=pl.Buffered(1)),
                pl.BlockSpec((far_total, share, BLK), lambda i, *_: (0, 0, 0), pipeline_mode=pl.Buffered(1)),
                pl.BlockSpec((group, slots, BLK, BLK), lambda i, *_: (i, 0, 0, 0)),
            ],
            out_specs=pl.BlockSpec((group, share, BLK), lambda i, *_: (i, 0, 0)),
            scratch_shapes=[pltpu.VMEM((block_total + far_total, share, BLK), jnp.bfloat16)],
        ),
        out_shape=jax.ShapeDtypeStruct(blocked.shape, jnp.bfloat16),
        compiler_params=pltpu.CompilerParams(vmem_limit_bytes=VMEM_LIMIT),
        name="pedigree",
    )(rel_index, rel_count, blocked, incoming, rel_prec)


def backward_kernel(scale, devices, place_ref, geno_ref, *refs):
    shares, (low_ref, high_ref, effects) = refs[:devices], refs[devices:]
    half = low_ref.shape[1]
    blocks, share, _ = shares[0].shape

    @pl.when(pl.program_id(0) == 0)
    def _():
        for shift in range(devices):
            origin = lax.rem(place_ref[0] + devices - shift, devices)
            first = pl.multiple_of(origin * share, share)
            for b in range(blocks):
                effects[pl.ds(first, share), b * BLK : (b + 1) * BLK] = shares[shift][b]

    product = scale * jnp.dot(effects[...], geno_ref[...], preferred_element_type=jnp.float32).T
    low_ref[...] = product[:, :half]
    high_ref[...] = product[:, half:]


def backward_product(genotypes, shares, place, scale):
    rows, width = genotypes.shape
    devices = len(shares)
    cols = devices * shares[0].shape[1]
    tile = divisor(width, 2 * BLK, 5 * BLK)
    return pl.pallas_call(
        functools.partial(backward_kernel, scale, devices),
        grid_spec=pltpu.PrefetchScalarGridSpec(
            num_scalar_prefetch=1,
            grid=(width // tile,),
            in_specs=[pl.BlockSpec((rows, tile), lambda i, *_: (0, i))]
            + [pl.BlockSpec(s.shape, lambda i, *_: (0, 0, 0), pipeline_mode=pl.Buffered(1)) for s in shares],
            out_specs=[pl.BlockSpec((tile, cols // 2), lambda i, *_: (i, 0))] * 2,
            scratch_shapes=[pltpu.VMEM((cols, rows), jnp.bfloat16)],
        ),
        out_shape=[jax.ShapeDtypeStruct((width, cols // 2), jnp.float32)] * 2,
        compiler_params=pltpu.CompilerParams(vmem_limit_bytes=VMEM_LIMIT),
        cost_estimate=pl.CostEstimate(
            flops=2 * rows * width * cols,
            bytes_accessed=2 * rows * (width + cols) + 4 * width * cols,
            transcendentals=0,
        ),
        name="backward_product",
    )(place, genotypes, *shares)


def turn(value, devices, shift):
    return lax.ppermute(value, "marker", [(d, (d + shift) % devices) for d in range(devices)])


def halving_sum(blocks, devices, bits):
    levels = devices.bit_length() - 1
    here = lax.axis_index("animal")
    total = blocks.reshape((2,) * levels + blocks.shape[1:])
    left = list(range(levels - 1, -1, -1))
    for bit in bits:
        axis = left.index(bit)
        mine = (here >> bit) & 1
        sent = lax.dynamic_index_in_dim(total, 1 - mine, axis, keepdims=False)
        kept = lax.dynamic_index_in_dim(total, mine, axis, keepdims=False)
        pairs = [(d, d ^ (1 << bit)) for d in range(devices)]
        got = lax.ppermute(sent.astype(jnp.bfloat16), "animal", pairs)
        total = kept + got.astype(jnp.float32)
        left.pop(axis)
    return total


def local(genotypes, direction, ridge, send_list, rel_index, rel_count, rel_prec):
    rows, width = genotypes.shape
    half = direction.shape[1] // 2
    groups = lax.axis_size("animal")
    devices = lax.axis_size("marker")
    place = lax.axis_index("marker").reshape(1)
    parts = 2
    part_rows = rows // parts
    tile = divisor(part_rows, BLK, 4 * BLK)

    owns, coded = [], [[] for _ in range(1, devices)]
    for part in range(parts):
        own, *sent = forward_product(
            genotypes, direction, place, devices, 1.0 / math.sqrt(MARKERS), part * part_rows, part_rows, tile
        )
        owns.append(own)
        for shift in range(1, devices):
            coded[shift - 1].append(turn(sent[shift - 1], devices, shift))
    own, outgoing = settle(owns, coded, send_list, tile // BLK)

    share = own.shape[1]
    outgoing = outgoing.reshape(groups, -1, share, BLK)
    incoming = lax.all_to_all(outgoing, "animal", split_axis=0, concat_axis=0, tiled=True)
    incoming = incoming.reshape(-1, share, BLK)
    relative = pedigree(own, incoming, rel_index, rel_count, rel_prec)
    shares = [relative] + [turn(relative, devices, shift) for shift in range(1, devices)]

    own_rows = width // groups
    low, high = [
        product.reshape(groups, own_rows, half)
        for product in backward_product(genotypes, shares, place, 1.0 / math.sqrt(groups * rows))
    ]
    levels = list(range(groups.bit_length() - 1))
    gradient = jnp.concatenate(
        [
            halving_sum(low, groups, levels),
            halving_sum(high, groups, levels[:1] + levels[:0:-1]),
        ],
        axis=1,
    )
    start = lax.axis_index("animal") * own_rows
    own_ridge = lax.dynamic_slice_in_dim(ridge, start, own_rows, 0)
    own_direction = lax.dynamic_slice_in_dim(direction, start, own_rows, 0)
    return gradient + own_ridge[:, None] * own_direction.astype(jnp.float32)


def solution(mesh):
    in_specs = (
        P("animal", "marker"),
        P("marker", None),
        P("marker"),
        P("animal", None, None),
        P("animal", None),
        P("animal"),
        P("animal", None, None, None),
    )
    out_specs = P(("marker", "animal"), None)
    return jax.shard_map(local, mesh=mesh, in_specs=in_specs, out_specs=out_specs, check_vma=False)
```

```python
import functools
import math

import jax
import jax.numpy as jnp
from jax import lax
from jax.experimental import pallas as pl
from jax.experimental.pallas import tpu as pltpu
from jax.sharding import PartitionSpec as P

MARKERS = 25600
BLK = 128
MARK = 16
VMEM_LIMIT = 56 * 1024 * 1024


def divisor(total, unit, most):
    best = unit
    for size in range(unit, most + 1, unit):
        if total % size == 0:
            best = size
    return best


def forward_kernel(scale, devices, place_ref, geno_ref, direction_ref, own_ref, *rest):
    sent, turned = rest[:-1], rest[-1]
    blocks, share, _ = own_ref.shape
    middle = geno_ref.shape[0] // 2
    product = scale * jnp.concatenate(
        [
            jnp.dot(geno_ref[rows, :], direction_ref[...], preferred_element_type=jnp.float32)
            for rows in (slice(0, middle), slice(middle, None))
        ],
        axis=0,
    )
    largest = jnp.max(jnp.abs(product), axis=(0, 1), keepdims=True)
    power = jnp.clip(jnp.ceil(jnp.log2(largest)), -100.0, 120.0)
    grow = jnp.exp2(14.0 - power)
    turned[...] = product.T
    for shift in range(devices):
        first = pl.multiple_of(lax.rem(place_ref[0] + shift, devices) * share, share)
        for b in range(blocks):
            piece = turned[pl.ds(first, share), b * BLK : (b + 1) * BLK]
            if shift == 0:
                own_ref[b] = piece
            else:
                coded = jnp.round(piece * grow).astype(jnp.int32).astype(jnp.int16)
                sent[shift - 1][b * share : (b + 1) * share] = coded
        if shift > 0:
            mark = jnp.broadcast_to(power, (MARK, BLK)).astype(jnp.int32).astype(jnp.int16)
            sent[shift - 1][blocks * share :] = mark


def forward_product(genotypes, direction, place, devices, scale, first, rows, tile):
    depth, cols = direction.shape
    start = first // tile
    share = cols // devices
    blocks = tile // BLK
    coded = blocks * share + MARK
    steps = rows // tile
    return pl.pallas_call(
        functools.partial(forward_kernel, scale, devices),
        grid_spec=pltpu.PrefetchScalarGridSpec(
            num_scalar_prefetch=1,
            grid=(steps,),
            in_specs=[
                pl.BlockSpec((tile, depth), lambda i, *_: (start + i, 0)),
                pl.BlockSpec((depth, cols), lambda i, *_: (0, 0), pipeline_mode=pl.Buffered(1)),
            ],
            out_specs=[pl.BlockSpec((blocks, share, BLK), lambda i, *_: (i, 0, 0))]
            + [pl.BlockSpec((coded, BLK), lambda i, *_: (i, 0))] * (devices - 1),
            scratch_shapes=[pltpu.VMEM((cols, tile), jnp.float32)],
        ),
        out_shape=[jax.ShapeDtypeStruct((steps * blocks, share, BLK), jnp.float32)]
        + [jax.ShapeDtypeStruct((steps * coded, BLK), jnp.int16)] * (devices - 1),
        compiler_params=pltpu.CompilerParams(vmem_limit_bytes=VMEM_LIMIT),
        cost_estimate=pl.CostEstimate(
            flops=2 * rows * depth * cols,
            bytes_accessed=2 * (rows + cols) * depth + 2 * rows * cols,
            transcendentals=0,
        ),
        name="forward_product",
    )(place, genotypes, direction)


def settle_kernel(parts, blocks, list_ref, *refs):
    owns, coded, (sum_ref, out_ref) = refs[:parts], refs[parts:-2], refs[-2:]
    share = sum_ref.shape[1]
    size = blocks * share + MARK
    at = 0
    for part, own in enumerate(owns):
        for step in range(own.shape[0] // blocks):
            row = step * size
            total = own[step * blocks : (step + 1) * blocks]
            for ref in coded[part::parts]:
                power = ref[row + blocks * share : row + size].astype(jnp.float32)[:1]
                steps = ref[row : row + blocks * share].astype(jnp.float32)
                total = total + (steps * jnp.exp2(power - 14.0)).reshape(blocks, share, BLK)
            sum_ref[at : at + blocks] = total.astype(sum_ref.dtype)
            at += blocks
    for i in range(out_ref.shape[0]):
        out_ref[i] = sum_ref[list_ref[i]]


def settle(owns, coded, send_list, blocks):
    block_total = sum(own.shape[0] for own in owns)
    share = owns[0].shape[1]
    sends = send_list.size
    flat = [ref for one in coded for ref in one]
    return pl.pallas_call(
        functools.partial(settle_kernel, len(owns), blocks),
        grid_spec=pltpu.PrefetchScalarGridSpec(
            num_scalar_prefetch=1,
            grid=(1,),
            in_specs=[pl.BlockSpec(x.shape, lambda i, *_, n=x.ndim: (0,) * n) for x in (*owns, *flat)],
            out_specs=[
                pl.BlockSpec((block_total, share, BLK), lambda i, *_: (0, 0, 0)),
                pl.BlockSpec((sends, share, BLK), lambda i, *_: (0, 0, 0)),
            ],
        ),
        out_shape=[
            jax.ShapeDtypeStruct((block_total, share, BLK), jnp.bfloat16),
            jax.ShapeDtypeStruct((sends, share, BLK), jnp.bfloat16),
        ],
        compiler_params=pltpu.CompilerParams(vmem_limit_bytes=VMEM_LIMIT),
        name="settle",
    )(send_list.reshape(-1), *owns, *flat)


def pedigree_kernel(group, own_total, start, index_ref, count_ref, own_ref, far_ref, prec_ref, out_ref, table):
    step = pl.program_id(0)

    @pl.when(step == 0)
    def _():
        table[:own_total] = own_ref[...]
        table[own_total:] = far_ref[...]

    for b in range(group):
        block = start + step * group + b
        total = None
        for j in range(prec_ref.shape[1]):
            source = table[index_ref[block, j]]
            source = jnp.where(j < count_ref[block], source, jnp.zeros_like(source))
            term = lax.dot_general(
                source, prec_ref[b, j], (((1,), (1,)), ((), ())), preferred_element_type=jnp.float32
            )
            total = term if total is None else total + term
        out_ref[b] = total.astype(out_ref.dtype)


def pedigree(blocked, incoming, rel_index, rel_count, rel_prec, start, count):
    block_total, share, _ = blocked.shape
    far_total = incoming.shape[0]
    slots = rel_prec.shape[1]
    group = divisor(math.gcd(count, start), 1, 6)
    first = start // group
    return pl.pallas_call(
        functools.partial(pedigree_kernel, group, block_total, start),
        grid_spec=pltpu.PrefetchScalarGridSpec(
            num_scalar_prefetch=2,
            grid=(count // group,),
            in_specs=[
                pl.BlockSpec((block_total, share, BLK), lambda i, *_: (0, 0, 0), pipeline_mode=pl.Buffered(1)),
                pl.BlockSpec((far_total, share, BLK), lambda i, *_: (0, 0, 0), pipeline_mode=pl.Buffered(1)),
                pl.BlockSpec((group, slots, BLK, BLK), lambda i, *_: (first + i, 0, 0, 0)),
            ],
            out_specs=pl.BlockSpec((group, share, BLK), lambda i, *_: (i, 0, 0)),
            scratch_shapes=[pltpu.VMEM((block_total + far_total, share, BLK), jnp.bfloat16)],
        ),
        out_shape=jax.ShapeDtypeStruct((count, share, BLK), jnp.bfloat16),
        compiler_params=pltpu.CompilerParams(vmem_limit_bytes=VMEM_LIMIT),
        name="pedigree",
    )(rel_index, rel_count, blocked, incoming, rel_prec)


def backward_kernel(scale, devices, place_ref, geno_ref, *refs):
    shares, sums = refs[:devices], refs[devices:-3]
    low_ref, high_ref, effects = refs[-3:]
    half = low_ref.shape[1]
    blocks, share, _ = shares[0].shape

    @pl.when(pl.program_id(0) == 0)
    def _():
        for b in range(blocks):
            pieces = []
            for origin in range(devices):
                piece = shares[0][b]
                for shift in range(1, devices):
                    here = place_ref[0] == (origin + shift) % devices
                    piece = jnp.where(here, shares[shift][b], piece)
                pieces.append(piece)
            effects[b * BLK : (b + 1) * BLK, :] = jnp.concatenate(pieces, axis=0).T

    middle = geno_ref.shape[0] // 2
    product = scale * sum(
        lax.dot_general(
            geno_ref[rows, :], effects[rows, :], (((0,), (0,)), ((), ())), preferred_element_type=jnp.float32
        )
        for rows in (slice(0, middle), slice(middle, None))
    )
    low, high = product[:, :half], product[:, half:]
    if sums:
        low, high = low + sums[0][...], high + sums[1][...]
    low_ref[...] = low
    high_ref[...] = high


def backward_product(genotypes, shares, place, scale, part, sums=()):
    width = genotypes.shape[1]
    devices = len(shares)
    rows = shares[0].shape[0] * BLK
    cols = devices * shares[0].shape[1]
    tile = divisor(width, BLK, 5 * BLK)
    half = pl.BlockSpec((tile, cols // 2), lambda i, *_: (i, 0))
    return pl.pallas_call(
        functools.partial(backward_kernel, scale, devices),
        grid_spec=pltpu.PrefetchScalarGridSpec(
            num_scalar_prefetch=1,
            grid=(width // tile,),
            in_specs=[pl.BlockSpec((rows, tile), lambda i, *_: (part, i))]
            + [pl.BlockSpec(s.shape, lambda i, *_: (0, 0, 0), pipeline_mode=pl.Buffered(1)) for s in shares]
            + [half] * len(sums),
            out_specs=[half] * 2,
            scratch_shapes=[pltpu.VMEM((rows, cols), jnp.bfloat16)],
        ),
        out_shape=[jax.ShapeDtypeStruct((width, cols // 2), jnp.float32)] * 2,
        input_output_aliases={2 + devices + k: k for k in range(len(sums))},
        compiler_params=pltpu.CompilerParams(vmem_limit_bytes=VMEM_LIMIT),
        cost_estimate=pl.CostEstimate(
            flops=2 * rows * width * cols,
            bytes_accessed=2 * rows * (width + cols) + 4 * width * cols * (2 if sums else 1),
            transcendentals=0,
        ),
        name="backward_product",
    )(place, genotypes, *shares, *sums)


def turn(value, devices, shift):
    return lax.ppermute(value, "marker", [(d, (d + shift) % devices) for d in range(devices)])


def halving_sum(blocks, devices, bits):
    levels = devices.bit_length() - 1
    here = lax.axis_index("animal")
    total = blocks.reshape((2,) * levels + blocks.shape[1:])
    left = list(range(levels - 1, -1, -1))
    for bit in bits:
        axis = left.index(bit)
        mine = (here >> bit) & 1
        sent = lax.dynamic_index_in_dim(total, 1 - mine, axis, keepdims=False)
        kept = lax.dynamic_index_in_dim(total, mine, axis, keepdims=False)
        pairs = [(d, d ^ (1 << bit)) for d in range(devices)]
        got = lax.ppermute(sent.astype(jnp.bfloat16), "animal", pairs)
        total = kept + got.astype(jnp.float32)
        left.pop(axis)
    return total


def local(genotypes, direction, ridge, send_list, rel_index, rel_count, rel_prec):
    rows, width = genotypes.shape
    half = direction.shape[1] // 2
    groups = lax.axis_size("animal")
    devices = lax.axis_size("marker")
    place = lax.axis_index("marker").reshape(1)
    parts = 2
    part_rows = rows // parts
    tile = divisor(part_rows, BLK, 4 * BLK)

    owns, coded = [], [[] for _ in range(1, devices)]
    for part in range(parts):
        own, *sent = forward_product(
            genotypes, direction, place, devices, 1.0 / math.sqrt(MARKERS), part * part_rows, part_rows, tile
        )
        owns.append(own)
        for shift in range(1, devices):
            coded[shift - 1].append(turn(sent[shift - 1], devices, shift))
    own, outgoing = settle(owns, coded, send_list, tile // BLK)

    share = own.shape[1]
    outgoing = outgoing.reshape(groups, -1, share, BLK)
    incoming = lax.all_to_all(outgoing, "animal", split_axis=0, concat_axis=0, tiled=True)
    incoming = incoming.reshape(-1, share, BLK)
    part_blocks = part_rows // BLK
    shares = []
    for part in range(parts):
        relative = pedigree(own, incoming, rel_index, rel_count, rel_prec, part * part_blocks, part_blocks)
        shares.append([relative] + [turn(relative, devices, shift) for shift in range(1, devices)])

    own_rows = width // groups
    sums = ()
    for part in range(parts):
        sums = backward_product(genotypes, shares[part], place, 1.0 / math.sqrt(groups * rows), part, sums)
    low, high = [total.reshape(groups, own_rows, half) for total in sums]
    levels = list(range(groups.bit_length() - 1))
    gradient = jnp.concatenate(
        [
            halving_sum(low, groups, levels),
            halving_sum(high, groups, levels[:1] + levels[:0:-1]),
        ],
        axis=1,
    )
    start = lax.axis_index("animal") * own_rows
    own_ridge = lax.dynamic_slice_in_dim(ridge, start, own_rows, 0)
    own_direction = lax.dynamic_slice_in_dim(direction, start, own_rows, 0)
    return gradient + own_ridge[:, None] * own_direction.astype(jnp.float32)


def solution(mesh):
    in_specs = (
        P("animal", "marker"),
        P("marker", None),
        P("marker"),
        P("animal", None, None),
        P("animal", None),
        P("animal"),
        P("animal", None, None, None),
    )
    out_specs = P(("marker", "animal"), None)
    return jax.shard_map(local, mesh=mesh, in_specs=in_specs, out_specs=out_specs, check_vma=False)
```

```python
import functools
import math

import jax
import jax.numpy as jnp
from jax import lax
from jax.experimental import pallas as pl
from jax.experimental.pallas import tpu as pltpu
from jax.sharding import PartitionSpec as P

MARKERS = 25600
BLK = 128
MARK = 16
VMEM_LIMIT = 56 * 1024 * 1024


def divisor(total, unit, most):
    best = unit
    for size in range(unit, most + 1, unit):
        if total % size == 0:
            best = size
    return best


def forward_kernel(scale, devices, place_ref, upper_ref, lower_ref, direction_ref, own_ref, *rest):
    sent, turned = rest[:-1], rest[-1]
    blocks, share, _ = own_ref.shape
    product = scale * jnp.concatenate(
        [
            jnp.dot(geno_ref[...], direction_ref[...], preferred_element_type=jnp.float32)
            for geno_ref in (upper_ref, lower_ref)
        ],
        axis=0,
    )
    largest = jnp.max(jnp.abs(product), axis=(0, 1), keepdims=True)
    power = jnp.clip(jnp.ceil(jnp.log2(largest)), -100.0, 120.0)
    grow = jnp.exp2(14.0 - power)
    turned[...] = product.T
    for shift in range(devices):
        first = pl.multiple_of(lax.rem(place_ref[0] + shift, devices) * share, share)
        for b in range(blocks):
            piece = turned[pl.ds(first, share), b * BLK : (b + 1) * BLK]
            if shift == 0:
                own_ref[b] = piece
            else:
                coded = jnp.round(piece * grow).astype(jnp.int32).astype(jnp.int16)
                sent[shift - 1][b * share : (b + 1) * share] = coded
        if shift > 0:
            mark = jnp.broadcast_to(power, (MARK, BLK)).astype(jnp.int32).astype(jnp.int16)
            sent[shift - 1][blocks * share :] = mark


def forward_product(genotypes, direction, place, devices, scale, first, rows, tile):
    depth, cols = direction.shape
    start = first // tile
    share = cols // devices
    blocks = tile // BLK
    coded = blocks * share + MARK
    steps = rows // tile
    return pl.pallas_call(
        functools.partial(forward_kernel, scale, devices),
        grid_spec=pltpu.PrefetchScalarGridSpec(
            num_scalar_prefetch=1,
            grid=(steps,),
            in_specs=[
                pl.BlockSpec((tile // 2, depth), lambda i, *_: (2 * (start + i), 0)),
                pl.BlockSpec((tile // 2, depth), lambda i, *_: (2 * (start + i) + 1, 0)),
                pl.BlockSpec((depth, cols), lambda i, *_: (0, 0), pipeline_mode=pl.Buffered(1)),
            ],
            out_specs=[pl.BlockSpec((blocks, share, BLK), lambda i, *_: (i, 0, 0))]
            + [pl.BlockSpec((coded, BLK), lambda i, *_: (i, 0))] * (devices - 1),
            scratch_shapes=[pltpu.VMEM((cols, tile), jnp.float32)],
        ),
        out_shape=[jax.ShapeDtypeStruct((steps * blocks, share, BLK), jnp.float32)]
        + [jax.ShapeDtypeStruct((steps * coded, BLK), jnp.int16)] * (devices - 1),
        compiler_params=pltpu.CompilerParams(vmem_limit_bytes=VMEM_LIMIT),
        cost_estimate=pl.CostEstimate(
            flops=2 * rows * depth * cols,
            bytes_accessed=2 * (rows + cols) * depth + 2 * rows * cols,
            transcendentals=0,
        ),
        name="forward_product",
    )(place, genotypes, genotypes, direction)


def settle_kernel(parts, blocks, list_ref, *refs):
    owns, coded, (sum_ref, out_ref) = refs[:parts], refs[parts:-2], refs[-2:]
    share = sum_ref.shape[1]
    size = blocks * share + MARK
    at = 0
    for part, own in enumerate(owns):
        for step in range(own.shape[0] // blocks):
            row = step * size
            total = own[step * blocks : (step + 1) * blocks]
            for ref in coded[part::parts]:
                power = ref[row + blocks * share : row + size].astype(jnp.float32)[:1]
                steps = ref[row : row + blocks * share].astype(jnp.float32)
                total = total + (steps * jnp.exp2(power - 14.0)).reshape(blocks, share, BLK)
            sum_ref[at : at + blocks] = total.astype(sum_ref.dtype)
            at += blocks
    for i in range(out_ref.shape[0]):
        out_ref[i] = sum_ref[list_ref[i]]


def settle(owns, coded, send_list, blocks):
    block_total = sum(own.shape[0] for own in owns)
    share = owns[0].shape[1]
    sends = send_list.size
    flat = [ref for one in coded for ref in one]
    return pl.pallas_call(
        functools.partial(settle_kernel, len(owns), blocks),
        grid_spec=pltpu.PrefetchScalarGridSpec(
            num_scalar_prefetch=1,
            grid=(1,),
            in_specs=[pl.BlockSpec(x.shape, lambda i, *_, n=x.ndim: (0,) * n) for x in (*owns, *flat)],
            out_specs=[
                pl.BlockSpec((block_total, share, BLK), lambda i, *_: (0, 0, 0)),
                pl.BlockSpec((sends, share, BLK), lambda i, *_: (0, 0, 0)),
            ],
        ),
        out_shape=[
            jax.ShapeDtypeStruct((block_total, share, BLK), jnp.bfloat16),
            jax.ShapeDtypeStruct((sends, share, BLK), jnp.bfloat16),
        ],
        compiler_params=pltpu.CompilerParams(vmem_limit_bytes=VMEM_LIMIT),
        name="settle",
    )(send_list.reshape(-1), *owns, *flat)


def pedigree_kernel(group, own_total, start, index_ref, count_ref, own_ref, far_ref, prec_ref, out_ref, table):
    step = pl.program_id(0)

    @pl.when(step == 0)
    def _():
        table[:own_total] = own_ref[...]
        table[own_total:] = far_ref[...]

    for b in range(group):
        block = start + step * group + b
        total = None
        for j in range(prec_ref.shape[1]):
            source = table[index_ref[block, j]]
            source = jnp.where(j < count_ref[block], source, jnp.zeros_like(source))
            term = lax.dot_general(
                source, prec_ref[b, j], (((1,), (1,)), ((), ())), preferred_element_type=jnp.float32
            )
            total = term if total is None else total + term
        out_ref[b] = total.astype(out_ref.dtype)


def pedigree(blocked, incoming, rel_index, rel_count, rel_prec, start, count):
    block_total, share, _ = blocked.shape
    far_total = incoming.shape[0]
    slots = rel_prec.shape[1]
    group = divisor(math.gcd(count, start), 1, 6)
    first = start // group
    return pl.pallas_call(
        functools.partial(pedigree_kernel, group, block_total, start),
        grid_spec=pltpu.PrefetchScalarGridSpec(
            num_scalar_prefetch=2,
            grid=(count // group,),
            in_specs=[
                pl.BlockSpec((block_total, share, BLK), lambda i, *_: (0, 0, 0), pipeline_mode=pl.Buffered(1)),
                pl.BlockSpec((far_total, share, BLK), lambda i, *_: (0, 0, 0), pipeline_mode=pl.Buffered(1)),
                pl.BlockSpec((group, slots, BLK, BLK), lambda i, *_: (first + i, 0, 0, 0)),
            ],
            out_specs=pl.BlockSpec((group, share, BLK), lambda i, *_: (i, 0, 0)),
            scratch_shapes=[pltpu.VMEM((block_total + far_total, share, BLK), jnp.bfloat16)],
        ),
        out_shape=jax.ShapeDtypeStruct((count, share, BLK), jnp.bfloat16),
        compiler_params=pltpu.CompilerParams(vmem_limit_bytes=VMEM_LIMIT),
        name="pedigree",
    )(rel_index, rel_count, blocked, incoming, rel_prec)


def backward_kernel(scale, devices, lanes, place_ref, *refs):
    geno, shares, sums = refs[:lanes], refs[lanes : lanes + devices], refs[lanes + devices : -3]
    low_ref, high_ref, effects = refs[-3:]
    half = low_ref.shape[1]
    blocks, share, _ = shares[0].shape

    @pl.when(pl.program_id(0) == 0)
    def _():
        for b in range(blocks):
            pieces = []
            for origin in range(devices):
                piece = shares[0][b]
                for shift in range(1, devices):
                    here = place_ref[0] == (origin + shift) % devices
                    piece = jnp.where(here, shares[shift][b], piece)
                pieces.append(piece)
            effects[b * BLK : (b + 1) * BLK, :] = jnp.concatenate(pieces, axis=0).T

    for lane, geno_ref in enumerate(geno):
        tile = geno_ref.shape[1]
        rows = slice(lane * tile, (lane + 1) * tile)
        product = scale * lax.dot_general(
            geno_ref[...], effects[...], (((0,), (0,)), ((), ())), preferred_element_type=jnp.float32
        )
        low, high = product[:, :half], product[:, half:]
        if sums:
            low, high = low + sums[0][rows, :], high + sums[1][rows, :]
        low_ref[rows, :] = low.astype(low_ref.dtype)
        high_ref[rows, :] = high.astype(high_ref.dtype)


def backward_product(genotypes, shares, place, scale, part, kind, sums=()):
    width = genotypes.shape[1]
    devices = len(shares)
    rows = shares[0].shape[0] * BLK
    cols = devices * shares[0].shape[1]
    lanes = 2 if width % (2 * BLK) == 0 else 1
    tile = divisor(width // lanes, BLK, 5 * BLK)
    half = pl.BlockSpec((lanes * tile, cols // 2), lambda i, *_: (i, 0))
    return pl.pallas_call(
        functools.partial(backward_kernel, scale, devices, lanes),
        grid_spec=pltpu.PrefetchScalarGridSpec(
            num_scalar_prefetch=1,
            grid=(width // (lanes * tile),),
            in_specs=[pl.BlockSpec((rows, tile), lambda i, *_, k=k: (part, lanes * i + k)) for k in range(lanes)]
            + [pl.BlockSpec(s.shape, lambda i, *_: (0, 0, 0), pipeline_mode=pl.Buffered(1)) for s in shares]
            + [half] * len(sums),
            out_specs=[half] * 2,
            scratch_shapes=[pltpu.VMEM((rows, cols), jnp.bfloat16)],
        ),
        out_shape=[jax.ShapeDtypeStruct((width, cols // 2), kind)] * 2,
        compiler_params=pltpu.CompilerParams(vmem_limit_bytes=VMEM_LIMIT),
        cost_estimate=pl.CostEstimate(
            flops=2 * rows * width * cols,
            bytes_accessed=2 * rows * (width + cols) + 4 * width * cols * (2 if sums else 1),
            transcendentals=0,
        ),
        name="backward_product",
    )(place, *[genotypes] * lanes, *shares, *sums)


def turn(value, devices, shift):
    return lax.ppermute(value, "marker", [(d, (d + shift) % devices) for d in range(devices)])


def halving_sum(blocks, devices, bits):
    levels = devices.bit_length() - 1
    here = lax.axis_index("animal")
    terms = [blocks.reshape((2,) * levels + blocks.shape[1:])]
    left = list(range(levels - 1, -1, -1))
    for bit in bits:
        axis = left.index(bit)
        mine = (here >> bit) & 1
        sent, kept = [
            [lax.dynamic_index_in_dim(term, side, axis, keepdims=False) for term in terms]
            for side in (1 - mine, mine)
        ]
        sent = sum(term.astype(jnp.float32) for term in sent).astype(jnp.bfloat16)
        terms = kept + [lax.ppermute(sent, "animal", [(d, d ^ (1 << bit)) for d in range(devices)])]
        left.pop(axis)
    return sum(term.astype(jnp.float32) for term in terms)


def local(genotypes, direction, ridge, send_list, rel_index, rel_count, rel_prec):
    rows, width = genotypes.shape
    half = direction.shape[1] // 2
    groups = lax.axis_size("animal")
    devices = lax.axis_size("marker")
    place = lax.axis_index("marker").reshape(1)
    parts = 2
    part_rows = rows // parts
    tile = divisor(part_rows, BLK, 4 * BLK)

    owns, coded = [], [[] for _ in range(1, devices)]
    for part in range(parts):
        own, *sent = forward_product(
            genotypes, direction, place, devices, 1.0 / math.sqrt(MARKERS), part * part_rows, part_rows, tile
        )
        owns.append(own)
        if part > 0:
            sent, earlier = lax.optimization_barrier((sent, [one[-1] for one in coded]))
            for one, value in zip(coded, earlier):
                one[-1] = value
        for shift in range(1, devices):
            coded[shift - 1].append(turn(sent[shift - 1], devices, shift))
    own, outgoing = settle(owns, coded, send_list, tile // BLK)

    share = own.shape[1]
    outgoing = outgoing.reshape(groups, -1, share, BLK)
    incoming = lax.all_to_all(outgoing, "animal", split_axis=0, concat_axis=0, tiled=True)
    incoming = incoming.reshape(-1, share, BLK)
    part_blocks = part_rows // BLK
    shares = []
    for part in range(parts):
        relative = pedigree(own, incoming, rel_index, rel_count, rel_prec, part * part_blocks, part_blocks)
        shares.append([relative] + [turn(relative, devices, shift) for shift in range(1, devices)])

    own_rows = width // groups
    sums = ()
    for part in range(parts):
        kind = jnp.float32 if part < parts - 1 else jnp.bfloat16
        sums = backward_product(genotypes, shares[part], place, 1.0 / math.sqrt(groups * rows), part, kind, sums)
    low, high = [total.reshape(groups, own_rows, half) for total in sums]
    levels = list(range(groups.bit_length() - 1))
    gradient = jnp.concatenate(
        [
            halving_sum(low, groups, levels),
            halving_sum(high, groups, levels[:1] + levels[:0:-1]),
        ],
        axis=1,
    )
    start = lax.axis_index("animal") * own_rows
    own_ridge = lax.dynamic_slice_in_dim(ridge, start, own_rows, 0)
    own_direction = lax.dynamic_slice_in_dim(direction, start, own_rows, 0)
    return gradient + own_ridge[:, None] * own_direction.astype(jnp.float32)


def solution(mesh):
    in_specs = (
        P("animal", "marker"),
        P("marker", None),
        P("marker"),
        P("animal", None, None),
        P("animal", None),
        P("animal"),
        P("animal", None, None, None),
    )
    out_specs = P(("marker", "animal"), None)
    return jax.shard_map(local, mesh=mesh, in_specs=in_specs, out_specs=out_specs, check_vma=False)
```

```python
import functools
import math

import jax
import jax.numpy as jnp
from jax import lax
from jax.experimental import pallas as pl
from jax.experimental.pallas import tpu as pltpu
from jax.sharding import PartitionSpec as P

MARKERS = 25600
BLK = 128
MARK = 16
VMEM_LIMIT = 56 * 1024 * 1024


def divisor(total, unit, most):
    best = unit
    for size in range(unit, most + 1, unit):
        if total % size == 0:
            best = size
    return best


def forward_kernel(scale, devices, place_ref, upper_ref, lower_ref, direction_ref, own_ref, sent_ref, turned):
    blocks, share, _ = own_ref.shape
    product = scale * jnp.concatenate(
        [
            jnp.dot(geno_ref[...], direction_ref[...], preferred_element_type=jnp.float32)
            for geno_ref in (upper_ref, lower_ref)
        ],
        axis=0,
    )
    largest = jnp.max(jnp.abs(product), axis=(0, 1), keepdims=True)
    power = jnp.clip(jnp.ceil(jnp.log2(largest)), -100.0, 120.0)
    grow = jnp.exp2(14.0 - power)
    turned[...] = product.T
    first = pl.multiple_of(place_ref[0] * share, share)
    mark = jnp.broadcast_to(power, (MARK, BLK)).astype(jnp.int32).astype(jnp.int16)
    for b in range(blocks):
        columns = slice(b * BLK, (b + 1) * BLK)
        own_ref[b] = turned[pl.ds(first, share), columns]
        for target in range(devices):
            piece = turned[target * share : (target + 1) * share, columns]
            coded = jnp.round(piece * grow).astype(jnp.int32).astype(jnp.int16)
            sent_ref[target, b * share : (b + 1) * share] = coded
    for target in range(devices):
        sent_ref[target, blocks * share :] = mark


def forward_product(genotypes, direction, place, devices, scale, first, rows, tile):
    depth, cols = direction.shape
    start = first // tile
    share = cols // devices
    blocks = tile // BLK
    coded = blocks * share + MARK
    steps = rows // tile
    return pl.pallas_call(
        functools.partial(forward_kernel, scale, devices),
        grid_spec=pltpu.PrefetchScalarGridSpec(
            num_scalar_prefetch=1,
            grid=(steps,),
            in_specs=[
                pl.BlockSpec((tile // 2, depth), lambda i, *_: (2 * (start + i), 0)),
                pl.BlockSpec((tile // 2, depth), lambda i, *_: (2 * (start + i) + 1, 0)),
                pl.BlockSpec((depth, cols), lambda i, *_: (0, 0), pipeline_mode=pl.Buffered(1)),
            ],
            out_specs=[
                pl.BlockSpec((blocks, share, BLK), lambda i, *_: (i, 0, 0)),
                pl.BlockSpec((devices, coded, BLK), lambda i, *_: (0, i, 0)),
            ],
            scratch_shapes=[pltpu.VMEM((cols, tile), jnp.float32)],
        ),
        out_shape=[
            jax.ShapeDtypeStruct((steps * blocks, share, BLK), jnp.float32),
            jax.ShapeDtypeStruct((devices, steps * coded, BLK), jnp.int16),
        ],
        compiler_params=pltpu.CompilerParams(vmem_limit_bytes=VMEM_LIMIT),
        cost_estimate=pl.CostEstimate(
            flops=2 * rows * depth * cols,
            bytes_accessed=2 * (rows + cols) * depth + 2 * rows * cols,
            transcendentals=0,
        ),
        name="forward_product",
    )(place, genotypes, genotypes, direction)


def settle_kernel(parts, blocks, list_ref, place_ref, *refs):
    owns, coded, (sum_ref, out_ref) = refs[:parts], refs[parts:-2], refs[-2:]
    share = sum_ref.shape[1]
    size = blocks * share + MARK
    at = 0
    for own, ref in zip(owns, coded):
        for step in range(own.shape[0] // blocks):
            row = step * size
            total = own[step * blocks : (step + 1) * blocks]
            for source in range(ref.shape[0]):
                power = ref[source, row + blocks * share : row + size].astype(jnp.float32)[:1]
                steps = ref[source, row : row + blocks * share].astype(jnp.float32)
                factor = jnp.where(place_ref[0] == source, 0.0, jnp.exp2(power - 14.0))
                total = total + (steps * factor).reshape(blocks, share, BLK)
            sum_ref[at : at + blocks] = total.astype(sum_ref.dtype)
            at += blocks
    for i in range(out_ref.shape[0]):
        out_ref[i] = sum_ref[list_ref[i]]


def settle(owns, coded, send_list, place, blocks):
    block_total = sum(own.shape[0] for own in owns)
    share = owns[0].shape[1]
    sends = send_list.size
    return pl.pallas_call(
        functools.partial(settle_kernel, len(owns), blocks),
        grid_spec=pltpu.PrefetchScalarGridSpec(
            num_scalar_prefetch=2,
            grid=(1,),
            in_specs=[pl.BlockSpec(x.shape, lambda i, *_: (0, 0, 0)) for x in (*owns, *coded)],
            out_specs=[
                pl.BlockSpec((block_total, share, BLK), lambda i, *_: (0, 0, 0)),
                pl.BlockSpec((sends, share, BLK), lambda i, *_: (0, 0, 0)),
            ],
        ),
        out_shape=[
            jax.ShapeDtypeStruct((block_total, share, BLK), jnp.bfloat16),
            jax.ShapeDtypeStruct((sends, share, BLK), jnp.bfloat16),
        ],
        compiler_params=pltpu.CompilerParams(vmem_limit_bytes=VMEM_LIMIT),
        name="settle",
    )(send_list.reshape(-1), place, *owns, *coded)


def pedigree_kernel(group, own_total, start, index_ref, count_ref, own_ref, far_ref, prec_ref, out_ref, table):
    step = pl.program_id(0)

    @pl.when(step == 0)
    def _():
        table[:own_total] = own_ref[...]
        table[own_total:] = far_ref[...]

    for b in range(group):
        block = start + step * group + b
        total = None
        for j in range(prec_ref.shape[1]):
            source = table[index_ref[block, j]]
            source = jnp.where(j < count_ref[block], source, jnp.zeros_like(source))
            term = lax.dot_general(
                source, prec_ref[b, j], (((1,), (1,)), ((), ())), preferred_element_type=jnp.float32
            )
            total = term if total is None else total + term
        out_ref[b] = total.astype(out_ref.dtype)


def pedigree(blocked, incoming, rel_index, rel_count, rel_prec, start, count):
    block_total, share, _ = blocked.shape
    far_total = incoming.shape[0]
    slots = rel_prec.shape[1]
    group = divisor(math.gcd(count, start), 1, 6)
    first = start // group
    return pl.pallas_call(
        functools.partial(pedigree_kernel, group, block_total, start),
        grid_spec=pltpu.PrefetchScalarGridSpec(
            num_scalar_prefetch=2,
            grid=(count // group,),
            in_specs=[
                pl.BlockSpec((block_total, share, BLK), lambda i, *_: (0, 0, 0), pipeline_mode=pl.Buffered(1)),
                pl.BlockSpec((far_total, share, BLK), lambda i, *_: (0, 0, 0), pipeline_mode=pl.Buffered(1)),
                pl.BlockSpec((group, slots, BLK, BLK), lambda i, *_: (first + i, 0, 0, 0)),
            ],
            out_specs=pl.BlockSpec((group, share, BLK), lambda i, *_: (i, 0, 0)),
            scratch_shapes=[pltpu.VMEM((block_total + far_total, share, BLK), jnp.bfloat16)],
        ),
        out_shape=jax.ShapeDtypeStruct((count, share, BLK), jnp.bfloat16),
        compiler_params=pltpu.CompilerParams(vmem_limit_bytes=VMEM_LIMIT),
        name="pedigree",
    )(rel_index, rel_count, blocked, incoming, rel_prec)


def origin_share(devices, place, origin):
    away, middle = place - origin, devices // 2
    if away == 0:
        return "own"
    if abs(away) < middle:
        return ("near", away)
    return ("far", abs(away))


def spread(value, devices):
    middle = devices // 2
    everyone = range(devices)

    def send(what, pairs):
        return lax.ppermute(what, "marker", pairs)

    found = {"own": value}
    found["far", middle] = send(value, [(d, (d + middle) % devices) for d in everyone])
    for away in range(1, middle):
        found["near", away] = send(value, [(d, d + away) for d in everyone if d + away < devices])
        found["near", -away] = send(value, [(d, d - away) for d in everyone if d >= away])
    for more in range(1, devices - middle):
        up = [(d, d + more) for d in range(middle, devices) if d + more < devices]
        down = [(d, d - more) for d in range(middle) if d >= more]
        found["far", middle + more] = send(found["far", middle], up + down)
    return found


def backward_kernel(scale, devices, lanes, keys, place_ref, *refs):
    geno, refs = refs[:lanes], refs[lanes:]
    shares, refs = dict(zip(keys, refs)), refs[len(keys) :]
    sums, (out_ref, effects) = refs[:-2], refs[-2:]
    blocks = shares["own"].shape[0]

    @pl.when(pl.program_id(0) == 0)
    def _():
        for b in range(blocks):
            pieces = []
            for origin in range(devices):
                piece = shares[origin_share(devices, 0, origin)][b]
                for place in range(1, devices):
                    other = shares[origin_share(devices, place, origin)][b]
                    piece = jnp.where(place_ref[0] == place, other, piece)
                pieces.append(piece)
            effects[b * BLK : (b + 1) * BLK, :] = jnp.concatenate(pieces, axis=0).T

    for lane, geno_ref in enumerate(geno):
        tile = geno_ref.shape[1]
        rows = slice(lane * tile, (lane + 1) * tile)
        product = scale * lax.dot_general(
            geno_ref[...], effects[...], (((0,), (0,)), ((), ())), preferred_element_type=jnp.float32
        )
        for earlier in sums:
            product = product + earlier[rows, :]
        out_ref[rows, :] = product.astype(out_ref.dtype)


def backward_product(genotypes, shares, place, devices, scale, part, kind, sums=()):
    width = genotypes.shape[1]
    keys = list(shares)
    own = shares["own"]
    rows = own.shape[0] * BLK
    cols = devices * own.shape[1]
    lanes = 2 if width % (2 * BLK) == 0 else 1
    tile = divisor(width // lanes, BLK, 5 * BLK)
    out = pl.BlockSpec((lanes * tile, cols), lambda i, *_: (i, 0))
    return pl.pallas_call(
        functools.partial(backward_kernel, scale, devices, lanes, keys),
        grid_spec=pltpu.PrefetchScalarGridSpec(
            num_scalar_prefetch=1,
            grid=(width // (lanes * tile),),
            in_specs=[pl.BlockSpec((rows, tile), lambda i, *_, k=k: (part, lanes * i + k)) for k in range(lanes)]
            + [pl.BlockSpec(own.shape, lambda i, *_: (0, 0, 0), pipeline_mode=pl.Buffered(1))] * len(keys)
            + [out] * len(sums),
            out_specs=out,
            scratch_shapes=[pltpu.VMEM((rows, cols), jnp.bfloat16)],
        ),
        out_shape=jax.ShapeDtypeStruct((width, cols), kind),
        compiler_params=pltpu.CompilerParams(vmem_limit_bytes=VMEM_LIMIT),
        cost_estimate=pl.CostEstimate(
            flops=2 * rows * width * cols,
            bytes_accessed=2 * rows * (width + cols) + 4 * width * cols * (2 if sums else 1),
            transcendentals=0,
        ),
        name="backward_product",
    )(place, *[genotypes] * lanes, *[shares[key] for key in keys], *sums)


def scatter_sum(blocks, devices):
    here = lax.axis_index("animal")
    core, chip = here & 1, here >> 1
    pairs = blocks.reshape((devices // 2, 2) + blocks.shape[1:])
    sent = lax.dynamic_index_in_dim(pairs, 1 - core, 1, keepdims=False)
    kept = lax.dynamic_index_in_dim(pairs, core, 1, keepdims=False)
    got = lax.ppermute(sent, "animal", [(d, d ^ 1) for d in range(devices)])

    def total(owner):
        return sum(
            lax.dynamic_index_in_dim(term, owner, 0, keepdims=False).astype(jnp.float32) for term in (kept, got)
        )

    arrived = [
        lax.ppermute(
            total(chip ^ away).astype(blocks.dtype), "animal", [(d, d ^ (2 * away)) for d in range(devices)]
        )
        for away in range(devices // 2 - 1, 0, -1)
    ]
    return total(chip) + sum(value.astype(jnp.float32) for value in arrived)


def local(genotypes, direction, ridge, send_list, rel_index, rel_count, rel_prec):
    rows, width = genotypes.shape
    groups = lax.axis_size("animal")
    devices = lax.axis_size("marker")
    place = lax.axis_index("marker").reshape(1)
    parts = 2
    part_rows = rows // parts
    tile = divisor(part_rows, BLK, 4 * BLK)

    owns, coded = [], []
    for part in range(parts):
        own, sent = forward_product(
            genotypes, direction, place, devices, 1.0 / math.sqrt(MARKERS), part * part_rows, part_rows, tile
        )
        if part > 0:
            sent, coded[-1] = lax.optimization_barrier((sent, coded[-1]))
        owns.append(own)
        coded.append(lax.all_to_all(sent, "marker", split_axis=0, concat_axis=0, tiled=True))
    own, outgoing = settle(owns, coded, send_list, place, tile // BLK)

    share = own.shape[1]
    outgoing = outgoing.reshape(groups, -1, share, BLK)
    incoming = lax.all_to_all(outgoing, "animal", split_axis=0, concat_axis=0, tiled=True)
    incoming = incoming.reshape(-1, share, BLK)
    part_blocks = part_rows // BLK
    shares = []
    for part in range(parts):
        relative = pedigree(own, incoming, rel_index, rel_count, rel_prec, part * part_blocks, part_blocks)
        shares.append(spread(relative, devices))

    own_rows = width // groups
    scale = 1.0 / math.sqrt(groups * rows)
    sums = ()
    for part in range(parts):
        kind = jnp.float32 if part < parts - 1 else jnp.bfloat16
        sums = (backward_product(genotypes, shares[part], place, devices, scale, part, kind, sums),)
    gradient = scatter_sum(sums[0].reshape(groups, own_rows, -1), groups)
    start = lax.axis_index("animal") * own_rows
    own_ridge = lax.dynamic_slice_in_dim(ridge, start, own_rows, 0)
    own_direction = lax.dynamic_slice_in_dim(direction, start, own_rows, 0)
    return gradient + own_ridge[:, None] * own_direction.astype(jnp.float32)


def solution(mesh):
    in_specs = (
        P("animal", "marker"),
        P("marker", None),
        P("marker"),
        P("animal", None, None),
        P("animal", None),
        P("animal"),
        P("animal", None, None, None),
    )
    out_specs = P(("marker", "animal"), None)
    return jax.shard_map(local, mesh=mesh, in_specs=in_specs, out_specs=out_specs, check_vma=False)
```

```python
import functools
import math

import jax
import jax.numpy as jnp
from jax import lax
from jax.experimental import pallas as pl
from jax.experimental.pallas import tpu as pltpu
from jax.sharding import PartitionSpec as P

MARKERS = 25600
BLK = 128
MARK = 16
VMEM_LIMIT = 56 * 1024 * 1024


def divisor(total, unit, most):
    best = unit
    for size in range(unit, most + 1, unit):
        if total % size == 0:
            best = size
    return best


def forward_kernel(scale, devices, place_ref, upper_ref, lower_ref, direction_ref, own_ref, *rest):
    sent, turned = rest[:-1], rest[-1]
    blocks, share, _ = own_ref.shape
    product = scale * jnp.concatenate(
        [
            jnp.dot(geno_ref[...], direction_ref[...], preferred_element_type=jnp.float32)
            for geno_ref in (upper_ref, lower_ref)
        ],
        axis=0,
    )
    largest = jnp.max(jnp.abs(product), axis=(0, 1), keepdims=True)
    power = jnp.clip(jnp.ceil(jnp.log2(largest)), -100.0, 120.0)
    grow = jnp.exp2(14.0 - power)
    turned[...] = product.T
    for shift in range(devices):
        first = pl.multiple_of(lax.rem(place_ref[0] + shift, devices) * share, share)
        for b in range(blocks):
            piece = turned[pl.ds(first, share), b * BLK : (b + 1) * BLK]
            if shift == 0:
                own_ref[b] = piece
            else:
                coded = jnp.round(piece * grow).astype(jnp.int32).astype(jnp.int16)
                sent[shift - 1][b * share : (b + 1) * share] = coded
        if shift > 0:
            mark = jnp.broadcast_to(power, (MARK, BLK)).astype(jnp.int32).astype(jnp.int16)
            sent[shift - 1][blocks * share :] = mark


def forward_product(genotypes, direction, place, devices, scale, first, rows, tile):
    depth, cols = direction.shape
    start = first // tile
    share = cols // devices
    blocks = tile // BLK
    coded = blocks * share + MARK
    steps = rows // tile
    return pl.pallas_call(
        functools.partial(forward_kernel, scale, devices),
        grid_spec=pltpu.PrefetchScalarGridSpec(
            num_scalar_prefetch=1,
            grid=(steps,),
            in_specs=[
                pl.BlockSpec((tile // 2, depth), lambda i, *_: (2 * (start + i), 0)),
                pl.BlockSpec((tile // 2, depth), lambda i, *_: (2 * (start + i) + 1, 0)),
                pl.BlockSpec((depth, cols), lambda i, *_: (0, 0), pipeline_mode=pl.Buffered(1)),
            ],
            out_specs=[pl.BlockSpec((blocks, share, BLK), lambda i, *_: (i, 0, 0))]
            + [pl.BlockSpec((coded, BLK), lambda i, *_: (i, 0))] * (devices - 1),
            scratch_shapes=[pltpu.VMEM((cols, tile), jnp.float32)],
        ),
        out_shape=[jax.ShapeDtypeStruct((steps * blocks, share, BLK), jnp.float32)]
        + [jax.ShapeDtypeStruct((steps * coded, BLK), jnp.int16)] * (devices - 1),
        compiler_params=pltpu.CompilerParams(vmem_limit_bytes=VMEM_LIMIT),
        cost_estimate=pl.CostEstimate(
            flops=2 * rows * depth * cols,
            bytes_accessed=2 * (rows + cols) * depth + 2 * rows * cols,
            transcendentals=0,
        ),
        name="forward_product",
    )(place, genotypes, genotypes, direction)


def settle_kernel(parts, blocks, list_ref, *refs):
    owns, coded, (sum_ref, out_ref) = refs[:parts], refs[parts:-2], refs[-2:]
    share = sum_ref.shape[1]
    size = blocks * share + MARK
    at = 0
    for part, own in enumerate(owns):
        for step in range(own.shape[0] // blocks):
            row = step * size
            total = own[step * blocks : (step + 1) * blocks]
            for ref in coded[part::parts]:
                power = ref[row + blocks * share : row + size].astype(jnp.float32)[:1]
                steps = ref[row : row + blocks * share].astype(jnp.float32)
                total = total + (steps * jnp.exp2(power - 14.0)).reshape(blocks, share, BLK)
            sum_ref[at : at + blocks] = total.astype(sum_ref.dtype)
            at += blocks
    for i in range(out_ref.shape[0]):
        out_ref[i] = sum_ref[list_ref[i]]


def settle(owns, coded, send_list, blocks):
    block_total = sum(own.shape[0] for own in owns)
    share = owns[0].shape[1]
    sends = send_list.size
    flat = [ref for one in coded for ref in one]
    return pl.pallas_call(
        functools.partial(settle_kernel, len(owns), blocks),
        grid_spec=pltpu.PrefetchScalarGridSpec(
            num_scalar_prefetch=1,
            grid=(1,),
            in_specs=[pl.BlockSpec(x.shape, lambda i, *_, n=x.ndim: (0,) * n) for x in (*owns, *flat)],
            out_specs=[
                pl.BlockSpec((block_total, share, BLK), lambda i, *_: (0, 0, 0)),
                pl.BlockSpec((sends, share, BLK), lambda i, *_: (0, 0, 0)),
            ],
        ),
        out_shape=[
            jax.ShapeDtypeStruct((block_total, share, BLK), jnp.bfloat16),
            jax.ShapeDtypeStruct((sends, share, BLK), jnp.bfloat16),
        ],
        compiler_params=pltpu.CompilerParams(vmem_limit_bytes=VMEM_LIMIT),
        name="settle",
    )(send_list.reshape(-1), *owns, *flat)


def pedigree_kernel(group, own_total, start, index_ref, count_ref, own_ref, far_ref, prec_ref, out_ref, table):
    step = pl.program_id(0)

    @pl.when(step == 0)
    def _():
        table[:own_total] = own_ref[...]
        table[own_total:] = far_ref[...]

    for b in range(group):
        block = start + step * group + b
        total = None
        for j in range(prec_ref.shape[1]):
            source = table[index_ref[block, j]]
            source = jnp.where(j < count_ref[block], source, jnp.zeros_like(source))
            term = lax.dot_general(
                prec_ref[b, j], source, (((1,), (1,)), ((), ())), preferred_element_type=jnp.float32
            )
            total = term if total is None else total + term
        out_ref[b] = total.T.astype(out_ref.dtype)


def pedigree(blocked, incoming, rel_index, rel_count, rel_prec, start, count):
    block_total, share, _ = blocked.shape
    far_total = incoming.shape[0]
    slots = rel_prec.shape[1]
    group = divisor(math.gcd(count, start), 1, 6)
    first = start // group
    return pl.pallas_call(
        functools.partial(pedigree_kernel, group, block_total, start),
        grid_spec=pltpu.PrefetchScalarGridSpec(
            num_scalar_prefetch=2,
            grid=(count // group,),
            in_specs=[
                pl.BlockSpec((block_total, share, BLK), lambda i, *_: (0, 0, 0), pipeline_mode=pl.Buffered(1)),
                pl.BlockSpec((far_total, share, BLK), lambda i, *_: (0, 0, 0), pipeline_mode=pl.Buffered(1)),
                pl.BlockSpec((group, slots, BLK, BLK), lambda i, *_: (first + i, 0, 0, 0)),
            ],
            out_specs=pl.BlockSpec((group, share, BLK), lambda i, *_: (i, 0, 0)),
            scratch_shapes=[pltpu.VMEM((block_total + far_total, share, BLK), jnp.bfloat16)],
        ),
        out_shape=jax.ShapeDtypeStruct((count, share, BLK), jnp.bfloat16),
        compiler_params=pltpu.CompilerParams(vmem_limit_bytes=VMEM_LIMIT),
        name="pedigree",
    )(rel_index, rel_count, blocked, incoming, rel_prec)


def backward_kernel(scale, devices, lanes, place_ref, *refs):
    geno, shares, sums = refs[:lanes], refs[lanes : lanes + devices], refs[lanes + devices : -3]
    low_ref, high_ref, effects = refs[-3:]
    half = low_ref.shape[1]
    blocks, share, _ = shares[0].shape

    @pl.when(pl.program_id(0) == 0)
    def _():
        for b in range(blocks):
            pieces = []
            for origin in range(devices):
                piece = shares[0][b]
                for shift in range(1, devices):
                    here = place_ref[0] == (origin + shift) % devices
                    piece = jnp.where(here, shares[shift][b], piece)
                pieces.append(piece)
            effects[b * BLK : (b + 1) * BLK, :] = jnp.concatenate(pieces, axis=0).T

    for lane, geno_ref in enumerate(geno):
        tile = geno_ref.shape[1]
        rows = slice(lane * tile, (lane + 1) * tile)
        product = scale * lax.dot_general(
            geno_ref[...], effects[...], (((0,), (0,)), ((), ())), preferred_element_type=jnp.float32
        )
        low, high = product[:, :half], product[:, half:]
        if sums:
            low, high = low + sums[0][rows, :], high + sums[1][rows, :]
        low_ref[rows, :] = low.astype(low_ref.dtype)
        high_ref[rows, :] = high.astype(high_ref.dtype)


def backward_product(genotypes, shares, place, scale, part, kind, sums=()):
    width = genotypes.shape[1]
    devices = len(shares)
    rows = shares[0].shape[0] * BLK
    cols = devices * shares[0].shape[1]
    lanes = 2 if width % (2 * BLK) == 0 else 1
    tile = divisor(width // lanes, BLK, 5 * BLK)
    half = pl.BlockSpec((lanes * tile, cols // 2), lambda i, *_: (i, 0))
    return pl.pallas_call(
        functools.partial(backward_kernel, scale, devices, lanes),
        grid_spec=pltpu.PrefetchScalarGridSpec(
            num_scalar_prefetch=1,
            grid=(width // (lanes * tile),),
            in_specs=[pl.BlockSpec((rows, tile), lambda i, *_, k=k: (part, lanes * i + k)) for k in range(lanes)]
            + [pl.BlockSpec(s.shape, lambda i, *_: (0, 0, 0), pipeline_mode=pl.Buffered(1)) for s in shares]
            + [half] * len(sums),
            out_specs=[half] * 2,
            scratch_shapes=[pltpu.VMEM((rows, cols), jnp.bfloat16)],
        ),
        out_shape=[jax.ShapeDtypeStruct((width, cols // 2), kind)] * 2,
        compiler_params=pltpu.CompilerParams(vmem_limit_bytes=VMEM_LIMIT),
        cost_estimate=pl.CostEstimate(
            flops=2 * rows * width * cols,
            bytes_accessed=2 * rows * (width + cols) + 4 * width * cols * (2 if sums else 1),
            transcendentals=0,
        ),
        name="backward_product",
    )(place, *[genotypes] * lanes, *shares, *sums)


def turn(value, devices, shift):
    return lax.ppermute(value, "marker", [(d, (d + shift) % devices) for d in range(devices)])


def halving_sum(blocks, devices, bits):
    levels = devices.bit_length() - 1
    here = lax.axis_index("animal")
    terms = [blocks.reshape((2,) * levels + blocks.shape[1:])]
    left = list(range(levels - 1, -1, -1))
    for bit in bits:
        axis = left.index(bit)
        mine = (here >> bit) & 1
        sent, kept = [
            [lax.dynamic_index_in_dim(term, side, axis, keepdims=False) for term in terms]
            for side in (1 - mine, mine)
        ]
        sent = sum(term.astype(jnp.float32) for term in sent).astype(jnp.bfloat16)
        terms = kept + [lax.ppermute(sent, "animal", [(d, d ^ (1 << bit)) for d in range(devices)])]
        left.pop(axis)
    return sum(term.astype(jnp.float32) for term in terms)


def local(genotypes, direction, ridge, send_list, rel_index, rel_count, rel_prec):
    rows, width = genotypes.shape
    half = direction.shape[1] // 2
    groups = lax.axis_size("animal")
    devices = lax.axis_size("marker")
    place = lax.axis_index("marker").reshape(1)
    parts = 2
    part_rows = rows // parts
    tile = divisor(part_rows, BLK, 4 * BLK)

    owns, coded = [], [[] for _ in range(1, devices)]
    for part in range(parts):
        own, *sent = forward_product(
            genotypes, direction, place, devices, 1.0 / math.sqrt(MARKERS), part * part_rows, part_rows, tile
        )
        owns.append(own)
        if part > 0:
            sent, earlier = lax.optimization_barrier((sent, [one[-1] for one in coded]))
            for one, value in zip(coded, earlier):
                one[-1] = value
        for shift in range(1, devices):
            coded[shift - 1].append(turn(sent[shift - 1], devices, shift))
    own, outgoing = settle(owns, coded, send_list, tile // BLK)

    share = own.shape[1]
    outgoing = outgoing.reshape(groups, -1, share, BLK)
    incoming = lax.all_to_all(outgoing, "animal", split_axis=0, concat_axis=0, tiled=True)
    incoming = incoming.reshape(-1, share, BLK)
    part_blocks = part_rows // BLK
    shares = []
    for part in range(parts):
        relative = pedigree(own, incoming, rel_index, rel_count, rel_prec, part * part_blocks, part_blocks)
        part_shares = [relative, turn(relative, devices, 1)]
        if part > 0:
            relative, shares[-1] = lax.optimization_barrier((relative, shares[-1]))
        shares.append(part_shares + [turn(relative, devices, shift) for shift in range(2, devices)])

    own_rows = width // groups
    sums = ()
    for part in range(parts):
        kind = jnp.float32 if part < parts - 1 else jnp.bfloat16
        sums = backward_product(genotypes, shares[part], place, 1.0 / math.sqrt(groups * rows), part, kind, sums)
    low, high = [total.reshape(groups, own_rows, half) for total in sums]
    levels = list(range(groups.bit_length() - 1))
    gradient = jnp.concatenate(
        [
            halving_sum(low, groups, levels),
            halving_sum(high, groups, levels[:1] + levels[:0:-1]),
        ],
        axis=1,
    )
    start = lax.axis_index("animal") * own_rows
    own_ridge = lax.dynamic_slice_in_dim(ridge, start, own_rows, 0)
    own_direction = lax.dynamic_slice_in_dim(direction, start, own_rows, 0)
    return gradient + own_ridge[:, None] * own_direction.astype(jnp.float32)


def solution(mesh):
    in_specs = (
        P("animal", "marker"),
        P("marker", None),
        P("marker"),
        P("animal", None, None),
        P("animal", None),
        P("animal"),
        P("animal", None, None, None),
    )
    out_specs = P(("marker", "animal"), None)
    return jax.shard_map(local, mesh=mesh, in_specs=in_specs, out_specs=out_specs, check_vma=False)
```

```python
import functools
import math

import jax
import jax.numpy as jnp
from jax import lax
from jax.experimental import pallas as pl
from jax.experimental.pallas import tpu as pltpu
from jax.sharding import PartitionSpec as P

MARKERS = 25600
BLK = 128
MARK = 16
VMEM_LIMIT = 63 * 1024 * 1024


def divisor(total, unit, most):
    best = unit
    for size in range(unit, most + 1, unit):
        if total % size == 0:
            best = size
    return best


def forward_kernel(scale, devices, place_ref, upper_ref, lower_ref, direction_ref, own_ref, *rest):
    sent, turned = rest[:-1], rest[-1]
    blocks, share, _ = own_ref.shape
    product = scale * jnp.concatenate(
        [
            jnp.dot(geno_ref[...], direction_ref[...], preferred_element_type=jnp.float32)
            for geno_ref in (upper_ref, lower_ref)
        ],
        axis=0,
    )
    largest = jnp.max(jnp.abs(product), axis=(0, 1), keepdims=True)
    power = jnp.clip(jnp.ceil(jnp.log2(largest)), -100.0, 120.0)
    grow = jnp.exp2(14.0 - power)
    turned[...] = product.T
    for shift in range(devices):
        first = pl.multiple_of(lax.rem(place_ref[0] + shift, devices) * share, share)
        for b in range(blocks):
            piece = turned[pl.ds(first, share), b * BLK : (b + 1) * BLK]
            if shift == 0:
                own_ref[b] = piece
            else:
                coded = jnp.round(piece * grow).astype(jnp.int32).astype(jnp.int16)
                sent[shift - 1][b * share : (b + 1) * share] = coded
        if shift > 0:
            mark = jnp.broadcast_to(power, (MARK, BLK)).astype(jnp.int32).astype(jnp.int16)
            sent[shift - 1][blocks * share :] = mark


def forward_product(genotypes, direction, place, devices, scale, first, rows, tile):
    depth, cols = direction.shape
    start = first // tile
    share = cols // devices
    blocks = tile // BLK
    coded = blocks * share + MARK
    steps = rows // tile
    return pl.pallas_call(
        functools.partial(forward_kernel, scale, devices),
        grid_spec=pltpu.PrefetchScalarGridSpec(
            num_scalar_prefetch=1,
            grid=(steps,),
            in_specs=[
                pl.BlockSpec((tile // 2, depth), lambda i, *_: (2 * (start + i), 0)),
                pl.BlockSpec((tile // 2, depth), lambda i, *_: (2 * (start + i) + 1, 0)),
                pl.BlockSpec((depth, cols), lambda i, *_: (0, 0), pipeline_mode=pl.Buffered(1)),
            ],
            out_specs=[pl.BlockSpec((blocks, share, BLK), lambda i, *_: (i, 0, 0))]
            + [pl.BlockSpec((coded, BLK), lambda i, *_: (i, 0))] * (devices - 1),
            scratch_shapes=[pltpu.VMEM((cols, tile), jnp.float32)],
        ),
        out_shape=[jax.ShapeDtypeStruct((steps * blocks, share, BLK), jnp.float32)]
        + [jax.ShapeDtypeStruct((steps * coded, BLK), jnp.int16)] * (devices - 1),
        compiler_params=pltpu.CompilerParams(vmem_limit_bytes=VMEM_LIMIT),
        cost_estimate=pl.CostEstimate(
            flops=2 * rows * depth * cols,
            bytes_accessed=2 * (rows + cols) * depth + 2 * rows * cols,
            transcendentals=0,
        ),
        name="forward_product",
    )(place, genotypes, genotypes, direction)


def settle_kernel(parts, blocks, list_ref, *refs):
    owns, coded, (sum_ref, out_ref) = refs[:parts], refs[parts:-2], refs[-2:]
    share = sum_ref.shape[1]
    size = blocks * share + MARK
    at = 0
    for part, own in enumerate(owns):
        for step in range(own.shape[0] // blocks):
            row = step * size
            total = own[step * blocks : (step + 1) * blocks]
            for ref in coded[part::parts]:
                power = ref[row + blocks * share : row + size].astype(jnp.float32)[:1]
                steps = ref[row : row + blocks * share].astype(jnp.float32)
                total = total + (steps * jnp.exp2(power - 14.0)).reshape(blocks, share, BLK)
            sum_ref[at : at + blocks] = total.astype(sum_ref.dtype)
            at += blocks
    for i in range(out_ref.shape[0]):
        out_ref[i] = sum_ref[list_ref[i]]


def settle(owns, coded, send_list, blocks):
    block_total = sum(own.shape[0] for own in owns)
    share = owns[0].shape[1]
    sends = send_list.size
    flat = [ref for one in coded for ref in one]
    return pl.pallas_call(
        functools.partial(settle_kernel, len(owns), blocks),
        grid_spec=pltpu.PrefetchScalarGridSpec(
            num_scalar_prefetch=1,
            grid=(1,),
            in_specs=[pl.BlockSpec(x.shape, lambda i, *_, n=x.ndim: (0,) * n) for x in (*owns, *flat)],
            out_specs=[
                pl.BlockSpec((block_total, share, BLK), lambda i, *_: (0, 0, 0)),
                pl.BlockSpec((sends, share, BLK), lambda i, *_: (0, 0, 0)),
            ],
        ),
        out_shape=[
            jax.ShapeDtypeStruct((block_total, share, BLK), jnp.bfloat16),
            jax.ShapeDtypeStruct((sends, share, BLK), jnp.bfloat16),
        ],
        compiler_params=pltpu.CompilerParams(vmem_limit_bytes=VMEM_LIMIT),
        name="settle",
    )(send_list.reshape(-1), *owns, *flat)


def pedigree_kernel(group, own_total, start, index_ref, count_ref, own_ref, far_ref, prec_ref, out_ref, table):
    step = pl.program_id(0)

    @pl.when(step == 0)
    def _():
        table[:own_total] = own_ref[...]
        table[own_total:] = far_ref[...]

    for b in range(group):
        block = start + step * group + b
        total = None
        for j in range(prec_ref.shape[1]):
            source = table[index_ref[block, j]]
            source = jnp.where(j < count_ref[block], source, jnp.zeros_like(source))
            term = lax.dot_general(
                prec_ref[b, j], source, (((1,), (1,)), ((), ())), preferred_element_type=jnp.float32
            )
            total = term if total is None else total + term
        out_ref[b] = total.T.astype(out_ref.dtype)


def pedigree(blocked, incoming, rel_index, rel_count, rel_prec, start, count):
    block_total, share, _ = blocked.shape
    far_total = incoming.shape[0]
    slots = rel_prec.shape[1]
    group = divisor(math.gcd(count, start), 1, 6)
    first = start // group
    return pl.pallas_call(
        functools.partial(pedigree_kernel, group, block_total, start),
        grid_spec=pltpu.PrefetchScalarGridSpec(
            num_scalar_prefetch=2,
            grid=(count // group,),
            in_specs=[
                pl.BlockSpec((block_total, share, BLK), lambda i, *_: (0, 0, 0), pipeline_mode=pl.Buffered(1)),
                pl.BlockSpec((far_total, share, BLK), lambda i, *_: (0, 0, 0), pipeline_mode=pl.Buffered(1)),
                pl.BlockSpec((group, slots, BLK, BLK), lambda i, *_: (first + i, 0, 0, 0)),
            ],
            out_specs=pl.BlockSpec((group, share, BLK), lambda i, *_: (i, 0, 0)),
            scratch_shapes=[pltpu.VMEM((block_total + far_total, share, BLK), jnp.bfloat16)],
        ),
        out_shape=jax.ShapeDtypeStruct((count, share, BLK), jnp.bfloat16),
        compiler_params=pltpu.CompilerParams(vmem_limit_bytes=VMEM_LIMIT),
        name="pedigree",
    )(rel_index, rel_count, blocked, incoming, rel_prec)


def backward_kernel(scale, devices, lanes, place_ref, *refs):
    geno, shares, sums = refs[:lanes], refs[lanes : lanes + devices], refs[lanes + devices : -3]
    low_ref, high_ref, effects = refs[-3:]
    half = low_ref.shape[1]
    blocks, share, _ = shares[0].shape

    @pl.when(pl.program_id(0) == 0)
    def _():
        for b in range(blocks):
            pieces = []
            for origin in range(devices):
                piece = shares[0][b]
                for shift in range(1, devices):
                    here = place_ref[0] == (origin + shift) % devices
                    piece = jnp.where(here, shares[shift][b], piece)
                pieces.append(piece)
            effects[b * BLK : (b + 1) * BLK, :] = jnp.concatenate(pieces, axis=0).T

    for lane, geno_ref in enumerate(geno):
        tile = geno_ref.shape[1]
        rows = slice(lane * tile, (lane + 1) * tile)
        product = scale * lax.dot_general(
            geno_ref[...], effects[...], (((0,), (0,)), ((), ())), preferred_element_type=jnp.float32
        )
        low, high = product[:, :half], product[:, half:]
        if sums:
            low, high = low + sums[0][rows, :], high + sums[1][rows, :]
        low_ref[rows, :] = low.astype(low_ref.dtype)
        high_ref[rows, :] = high.astype(high_ref.dtype)


def backward_product(genotypes, shares, place, scale, part, kind, sums=()):
    width = genotypes.shape[1]
    devices = len(shares)
    rows = shares[0].shape[0] * BLK
    cols = devices * shares[0].shape[1]
    lanes = 2 if width % (2 * BLK) == 0 else 1
    tile = divisor(width // lanes, BLK, 5 * BLK)
    half = pl.BlockSpec((lanes * tile, cols // 2), lambda i, *_: (i, 0))
    return pl.pallas_call(
        functools.partial(backward_kernel, scale, devices, lanes),
        grid_spec=pltpu.PrefetchScalarGridSpec(
            num_scalar_prefetch=1,
            grid=(width // (lanes * tile),),
            in_specs=[pl.BlockSpec((rows, tile), lambda i, *_, k=k: (part, lanes * i + k)) for k in range(lanes)]
            + [pl.BlockSpec(s.shape, lambda i, *_: (0, 0, 0), pipeline_mode=pl.Buffered(1)) for s in shares]
            + [half] * len(sums),
            out_specs=[half] * 2,
            scratch_shapes=[pltpu.VMEM((rows, cols), jnp.bfloat16)],
        ),
        out_shape=[jax.ShapeDtypeStruct((width, cols // 2), kind)] * 2,
        compiler_params=pltpu.CompilerParams(vmem_limit_bytes=VMEM_LIMIT),
        cost_estimate=pl.CostEstimate(
            flops=2 * rows * width * cols,
            bytes_accessed=2 * rows * (width + cols) + 4 * width * cols * (2 if sums else 1),
            transcendentals=0,
        ),
        name="backward_product",
    )(place, *[genotypes] * lanes, *shares, *sums)


def turn(value, devices, shift):
    return lax.ppermute(value, "marker", [(d, (d + shift) % devices) for d in range(devices)])


def combine_kernel(counts, index_ref, *refs):
    terms, outs = refs[: sum(counts)], refs[sum(counts) :]
    for count, out_ref in zip(counts, outs):
        total = sum(term[0].astype(jnp.float32) for term in terms[:count])
        out_ref[0] = total.astype(out_ref.dtype)
        terms = terms[count:]


def finish_kernel(counts, index_ref, ridge_ref, direction_ref, *refs):
    terms, out_ref = refs[:-1], refs[-1]
    half = out_ref.shape[1] // len(counts)
    for flow, count in enumerate(counts):
        columns = slice(flow * half, (flow + 1) * half)
        total = sum(term[0].astype(jnp.float32) for term in terms[:count])
        out_ref[:, columns] = total + ridge_ref[...] * direction_ref[0, :, columns].astype(jnp.float32)
        terms = terms[count:]


def combine(flows, places, blocks):
    terms = [term for flow in flows for term in flow]
    shape = terms[0].shape[1:]

    def at(k):
        return pl.BlockSpec((1,) + shape, lambda i, index: (index[k * blocks + i], 0, 0))

    return pl.pallas_call(
        functools.partial(combine_kernel, [len(flow) for flow in flows]),
        grid_spec=pltpu.PrefetchScalarGridSpec(
            num_scalar_prefetch=1,
            grid=(blocks,),
            in_specs=[at(k) for k in range(len(terms))],
            out_specs=[pl.BlockSpec((1,) + shape, lambda i, index: (i, 0, 0))] * len(flows),
        ),
        out_shape=[jax.ShapeDtypeStruct((blocks,) + shape, terms[0].dtype)] * len(flows),
        compiler_params=pltpu.CompilerParams(vmem_limit_bytes=VMEM_LIMIT),
        name="combine",
    )(places, *terms)


def finish(flows, places, own_ridge, direction, here):
    terms = [term for flow in flows for term in flow]
    shape = terms[0].shape[1:]
    cols = direction.shape[-1]
    last = len(terms)

    def at(k):
        return pl.BlockSpec((1,) + shape, lambda i, index: (index[k], 0, 0))

    return pl.pallas_call(
        functools.partial(finish_kernel, [len(flow) for flow in flows]),
        grid_spec=pltpu.PrefetchScalarGridSpec(
            num_scalar_prefetch=1,
            grid=(1,),
            in_specs=[
                pl.BlockSpec(own_ridge.shape, lambda i, index: (0, 0)),
                pl.BlockSpec((1, shape[0], cols), lambda i, index: (index[last], 0, 0)),
            ]
            + [at(k) for k in range(last)],
            out_specs=pl.BlockSpec((shape[0], cols), lambda i, index: (0, 0)),
        ),
        out_shape=jax.ShapeDtypeStruct((shape[0], cols), jnp.float32),
        compiler_params=pltpu.CompilerParams(vmem_limit_bytes=VMEM_LIMIT),
        name="finish",
    )(jnp.concatenate([places, here.reshape(1)]), own_ridge, direction, *terms)


def halving_sum(halves, devices, orders, own_ridge, direction):
    levels = devices.bit_length() - 1
    here = lax.axis_index("animal")
    every = list(range(levels - 1, -1, -1))
    terms = [[(half, every)] for half in halves]

    def place(bits, left, block, bit, side):
        index = jnp.int32(0)
        for b in bits:
            if b in left:
                value = (block >> (len(left) - 1 - left.index(b))) & 1
            else:
                value = (here >> b) & 1
                if b == bit:
                    value = value ^ side
            index = index * 2 + value
        return index

    for step in range(levels):
        lefts = [[b for b in every if b not in order[: step + 1]] for order in orders]
        blocks = 1 << (levels - 1 - step)
        places = jnp.stack(
            [
                place(bits, left, block, order[step], 1)
                for flow, left, order in zip(terms, lefts, orders)
                for _, bits in flow
                for block in range(blocks)
            ]
        )
        sent = combine([[array for array, _ in flow] for flow in terms], places, blocks)
        for flow, left, order, value in zip(terms, lefts, orders, sent):
            pairs = [(d, d ^ (1 << order[step])) for d in range(devices)]
            flow.append((lax.ppermute(value, "animal", pairs), left))
    places = jnp.stack([place(bits, [], 0, None, 0) for flow in terms for _, bits in flow])
    return finish([[array for array, _ in flow] for flow in terms], places, own_ridge, direction, here)


def local(genotypes, direction, ridge, send_list, rel_index, rel_count, rel_prec):
    rows, width = genotypes.shape
    half = direction.shape[1] // 2
    groups = lax.axis_size("animal")
    devices = lax.axis_size("marker")
    place = lax.axis_index("marker").reshape(1)
    parts = 2
    part_rows = rows // parts
    tile = divisor(part_rows, BLK, 4 * BLK)

    owns, coded = [], [[] for _ in range(1, devices)]
    for part in range(parts):
        own, *sent = forward_product(
            genotypes, direction, place, devices, 1.0 / math.sqrt(MARKERS), part * part_rows, part_rows, tile
        )
        owns.append(own)
        if part > 0:
            sent, earlier = lax.optimization_barrier((sent, [one[-1] for one in coded]))
            for one, value in zip(coded, earlier):
                one[-1] = value
        for shift in range(1, devices):
            coded[shift - 1].append(turn(sent[shift - 1], devices, shift))
    own, outgoing = settle(owns, coded, send_list, tile // BLK)

    share = own.shape[1]
    outgoing = outgoing.reshape(groups, -1, share, BLK)
    incoming = lax.all_to_all(outgoing, "animal", split_axis=0, concat_axis=0, tiled=True)
    incoming = incoming.reshape(-1, share, BLK)
    part_blocks = part_rows // BLK
    shares = []
    for part in range(parts):
        relative = pedigree(own, incoming, rel_index, rel_count, rel_prec, part * part_blocks, part_blocks)
        shares.append([relative] + [turn(relative, devices, shift) for shift in range(1, devices)])

    own_rows = width // groups
    sums = ()
    for part in range(parts):
        kind = jnp.float32 if part < parts - 1 else jnp.bfloat16
        sums = backward_product(genotypes, shares[part], place, 1.0 / math.sqrt(groups * rows), part, kind, sums)
    low, high = [total.reshape(groups, own_rows, half) for total in sums]
    levels = list(range(groups.bit_length() - 1))
    orders = [levels, levels[:1] + levels[:0:-1]]
    start = lax.axis_index("animal") * own_rows
    own_ridge = lax.dynamic_slice_in_dim(ridge, start, own_rows, 0).reshape(own_rows, 1)
    by_owner = direction.reshape(groups, own_rows, -1)
    return halving_sum([low, high], groups, orders, own_ridge, by_owner)


def solution(mesh):
    in_specs = (
        P("animal", "marker"),
        P("marker", None),
        P("marker"),
        P("animal", None, None),
        P("animal", None),
        P("animal"),
        P("animal", None, None, None),
    )
    out_specs = P(("marker", "animal"), None)
    return jax.shard_map(local, mesh=mesh, in_specs=in_specs, out_specs=out_specs, check_vma=False)
```

```python
import functools
import math

import jax
import jax.numpy as jnp
from jax import lax
from jax.experimental import pallas as pl
from jax.experimental.pallas import tpu as pltpu
from jax.sharding import PartitionSpec as P

MARKERS = 25600
BLK = 128
MARK = 16
VMEM_LIMIT = 63 * 1024 * 1024


def divisor(total, unit, most):
    best = unit
    for size in range(unit, most + 1, unit):
        if total % size == 0:
            best = size
    return best


def forward_kernel(scale, devices, place_ref, upper_ref, lower_ref, direction_ref, own_ref, *rest):
    sent, turned = rest[:-1], rest[-1]
    blocks, share, _ = own_ref.shape
    product = scale * jnp.concatenate(
        [
            jnp.dot(geno_ref[...], direction_ref[...], preferred_element_type=jnp.float32)
            for geno_ref in (upper_ref, lower_ref)
        ],
        axis=0,
    )
    largest = jnp.max(jnp.abs(product), axis=(0, 1), keepdims=True)
    power = jnp.clip(jnp.ceil(jnp.log2(largest)), -100.0, 120.0)
    grow = jnp.exp2(14.0 - power)
    turned[...] = product.T
    for shift in range(devices):
        first = pl.multiple_of(lax.rem(place_ref[0] + shift, devices) * share, share)
        for b in range(blocks):
            piece = turned[pl.ds(first, share), b * BLK : (b + 1) * BLK]
            if shift == 0:
                own_ref[b] = piece
            else:
                coded = jnp.round(piece * grow).astype(jnp.int32).astype(jnp.int16)
                sent[shift - 1][b * share : (b + 1) * share] = coded
        if shift > 0:
            mark = jnp.broadcast_to(power, (MARK, BLK)).astype(jnp.int32).astype(jnp.int16)
            sent[shift - 1][blocks * share :] = mark


def forward_product(genotypes, direction, place, devices, scale, first, rows, tile):
    depth, cols = direction.shape
    start = first // tile
    share = cols // devices
    blocks = tile // BLK
    coded = blocks * share + MARK
    steps = rows // tile
    return pl.pallas_call(
        functools.partial(forward_kernel, scale, devices),
        grid_spec=pltpu.PrefetchScalarGridSpec(
            num_scalar_prefetch=1,
            grid=(steps,),
            in_specs=[
                pl.BlockSpec((tile // 2, depth), lambda i, *_: (2 * (start + i), 0)),
                pl.BlockSpec((tile // 2, depth), lambda i, *_: (2 * (start + i) + 1, 0)),
                pl.BlockSpec((depth, cols), lambda i, *_: (0, 0), pipeline_mode=pl.Buffered(1)),
            ],
            out_specs=[pl.BlockSpec((blocks, share, BLK), lambda i, *_: (i, 0, 0))]
            + [pl.BlockSpec((coded, BLK), lambda i, *_: (i, 0))] * (devices - 1),
            scratch_shapes=[pltpu.VMEM((cols, tile), jnp.float32)],
        ),
        out_shape=[jax.ShapeDtypeStruct((steps * blocks, share, BLK), jnp.float32)]
        + [jax.ShapeDtypeStruct((steps * coded, BLK), jnp.int16)] * (devices - 1),
        compiler_params=pltpu.CompilerParams(vmem_limit_bytes=VMEM_LIMIT),
        cost_estimate=pl.CostEstimate(
            flops=2 * rows * depth * cols,
            bytes_accessed=2 * (rows + cols) * depth + 2 * rows * cols,
            transcendentals=0,
        ),
        name="forward_product",
    )(place, genotypes, genotypes, direction)


def settle_kernel(parts, blocks, list_ref, *refs):
    owns, coded, (sum_ref, out_ref) = refs[:parts], refs[parts:-2], refs[-2:]
    share = sum_ref.shape[1]
    size = blocks * share + MARK
    at = 0
    for part, own in enumerate(owns):
        for step in range(own.shape[0] // blocks):
            row = step * size
            total = own[step * blocks : (step + 1) * blocks]
            for ref in coded[part::parts]:
                power = ref[row + blocks * share : row + size].astype(jnp.float32)[:1]
                steps = ref[row : row + blocks * share].astype(jnp.float32)
                total = total + (steps * jnp.exp2(power - 14.0)).reshape(blocks, share, BLK)
            sum_ref[at : at + blocks] = total.astype(sum_ref.dtype)
            at += blocks
    for i in range(out_ref.shape[0]):
        out_ref[i] = sum_ref[list_ref[i]]


def settle(owns, coded, send_list, blocks):
    block_total = sum(own.shape[0] for own in owns)
    share = owns[0].shape[1]
    sends = send_list.size
    flat = [ref for one in coded for ref in one]
    return pl.pallas_call(
        functools.partial(settle_kernel, len(owns), blocks),
        grid_spec=pltpu.PrefetchScalarGridSpec(
            num_scalar_prefetch=1,
            grid=(1,),
            in_specs=[pl.BlockSpec(x.shape, lambda i, *_, n=x.ndim: (0,) * n) for x in (*owns, *flat)],
            out_specs=[
                pl.BlockSpec((block_total, share, BLK), lambda i, *_: (0, 0, 0)),
                pl.BlockSpec((sends, share, BLK), lambda i, *_: (0, 0, 0)),
            ],
        ),
        out_shape=[
            jax.ShapeDtypeStruct((block_total, share, BLK), jnp.bfloat16),
            jax.ShapeDtypeStruct((sends, share, BLK), jnp.bfloat16),
        ],
        compiler_params=pltpu.CompilerParams(vmem_limit_bytes=VMEM_LIMIT),
        name="settle",
    )(send_list.reshape(-1), *owns, *flat)


def pedigree_kernel(group, own_total, start, index_ref, count_ref, own_ref, far_ref, prec_ref, out_ref, table):
    step = pl.program_id(0)

    @pl.when(step == 0)
    def _():
        table[:own_total] = own_ref[...]
        table[own_total:] = far_ref[...]

    for b in range(group):
        block = start + step * group + b
        total = None
        for j in range(prec_ref.shape[1]):
            source = table[index_ref[block, j]]
            source = jnp.where(j < count_ref[block], source, jnp.zeros_like(source))
            term = lax.dot_general(
                prec_ref[b, j], source, (((1,), (1,)), ((), ())), preferred_element_type=jnp.float32
            )
            total = term if total is None else total + term
        out_ref[b] = total.T.astype(out_ref.dtype)


def pedigree(blocked, incoming, rel_index, rel_count, rel_prec, start, count):
    block_total, share, _ = blocked.shape
    far_total = incoming.shape[0]
    slots = rel_prec.shape[1]
    group = divisor(math.gcd(count, start), 1, 6)
    first = start // group
    return pl.pallas_call(
        functools.partial(pedigree_kernel, group, block_total, start),
        grid_spec=pltpu.PrefetchScalarGridSpec(
            num_scalar_prefetch=2,
            grid=(count // group,),
            in_specs=[
                pl.BlockSpec((block_total, share, BLK), lambda i, *_: (0, 0, 0), pipeline_mode=pl.Buffered(1)),
                pl.BlockSpec((far_total, share, BLK), lambda i, *_: (0, 0, 0), pipeline_mode=pl.Buffered(1)),
                pl.BlockSpec((group, slots, BLK, BLK), lambda i, *_: (first + i, 0, 0, 0)),
            ],
            out_specs=pl.BlockSpec((group, share, BLK), lambda i, *_: (i, 0, 0)),
            scratch_shapes=[pltpu.VMEM((block_total + far_total, share, BLK), jnp.bfloat16)],
        ),
        out_shape=jax.ShapeDtypeStruct((count, share, BLK), jnp.bfloat16),
        compiler_params=pltpu.CompilerParams(vmem_limit_bytes=VMEM_LIMIT),
        name="pedigree",
    )(rel_index, rel_count, blocked, incoming, rel_prec)


def backward_kernel(scale, devices, lanes, place_ref, *refs):
    geno, shares, sums = refs[:lanes], refs[lanes : lanes + devices], refs[lanes + devices : -3]
    low_ref, high_ref, effects = refs[-3:]
    half = low_ref.shape[1]
    blocks, share, _ = shares[0].shape

    @pl.when(pl.program_id(0) == 0)
    def _():
        for b in range(blocks):
            pieces = []
            for origin in range(devices):
                piece = shares[0][b]
                for shift in range(1, devices):
                    here = place_ref[0] == (origin + shift) % devices
                    piece = jnp.where(here, shares[shift][b], piece)
                pieces.append(piece)
            effects[b * BLK : (b + 1) * BLK, :] = jnp.concatenate(pieces, axis=0).T

    for lane, geno_ref in enumerate(geno):
        tile = geno_ref.shape[1]
        rows = slice(lane * tile, (lane + 1) * tile)
        product = scale * lax.dot_general(
            geno_ref[...], effects[...], (((0,), (0,)), ((), ())), preferred_element_type=jnp.float32
        )
        low, high = product[:, :half], product[:, half:]
        if sums:
            low, high = low + sums[0][rows, :], high + sums[1][rows, :]
        low_ref[rows, :] = low.astype(low_ref.dtype)
        high_ref[rows, :] = high.astype(high_ref.dtype)


def backward_product(genotypes, shares, place, scale, part, kind, sums=()):
    width = genotypes.shape[1]
    devices = len(shares)
    rows = shares[0].shape[0] * BLK
    cols = devices * shares[0].shape[1]
    lanes = 2 if width % (2 * BLK) == 0 else 1
    tile = divisor(width // lanes, BLK, 5 * BLK)
    half = pl.BlockSpec((lanes * tile, cols // 2), lambda i, *_: (i, 0))
    return pl.pallas_call(
        functools.partial(backward_kernel, scale, devices, lanes),
        grid_spec=pltpu.PrefetchScalarGridSpec(
            num_scalar_prefetch=1,
            grid=(width // (lanes * tile),),
            in_specs=[pl.BlockSpec((rows, tile), lambda i, *_, k=k: (part, lanes * i + k)) for k in range(lanes)]
            + [pl.BlockSpec(s.shape, lambda i, *_: (0, 0, 0), pipeline_mode=pl.Buffered(1)) for s in shares]
            + [half] * len(sums),
            out_specs=[half] * 2,
            scratch_shapes=[pltpu.VMEM((rows, cols), jnp.bfloat16)],
        ),
        out_shape=[jax.ShapeDtypeStruct((width, cols // 2), kind)] * 2,
        compiler_params=pltpu.CompilerParams(vmem_limit_bytes=VMEM_LIMIT),
        cost_estimate=pl.CostEstimate(
            flops=2 * rows * width * cols,
            bytes_accessed=2 * rows * (width + cols) + 4 * width * cols * (2 if sums else 1),
            transcendentals=0,
        ),
        name="backward_product",
    )(place, *[genotypes] * lanes, *shares, *sums)


def turn(value, devices, shift):
    return lax.ppermute(value, "marker", [(d, (d + shift) % devices) for d in range(devices)])


def halving_sum(blocks, devices, bits):
    levels = devices.bit_length() - 1
    here = lax.axis_index("animal")
    terms = [blocks.reshape((2,) * levels + blocks.shape[1:])]
    left = list(range(levels - 1, -1, -1))
    for bit in bits:
        axis = left.index(bit)
        mine = (here >> bit) & 1
        sent, kept = [
            [lax.dynamic_index_in_dim(term, side, axis, keepdims=False) for term in terms]
            for side in (1 - mine, mine)
        ]
        sent = sum(term.astype(jnp.float32) for term in sent).astype(jnp.bfloat16)
        terms = kept + [lax.ppermute(sent, "animal", [(d, d ^ (1 << bit)) for d in range(devices)])]
        left.pop(axis)
    return sum(term.astype(jnp.float32) for term in terms)


def local(genotypes, direction, ridge, send_list, rel_index, rel_count, rel_prec):
    rows, width = genotypes.shape
    half = direction.shape[1] // 2
    groups = lax.axis_size("animal")
    devices = lax.axis_size("marker")
    place = lax.axis_index("marker").reshape(1)
    parts = 2
    part_rows = rows // parts
    tile = divisor(part_rows, BLK, 4 * BLK)

    owns, coded = [], [[] for _ in range(1, devices)]
    for part in range(parts):
        own, *sent = forward_product(
            genotypes, direction, place, devices, 1.0 / math.sqrt(MARKERS), part * part_rows, part_rows, tile
        )
        owns.append(own)
        if part > 0:
            sent, earlier = lax.optimization_barrier((sent, [one[-1] for one in coded]))
            for one, value in zip(coded, earlier):
                one[-1] = value
        for shift in range(1, devices):
            coded[shift - 1].append(turn(sent[shift - 1], devices, shift))
    own, outgoing = settle(owns, coded, send_list, tile // BLK)

    share = own.shape[1]
    outgoing = outgoing.reshape(groups, -1, share, BLK)
    incoming = lax.all_to_all(outgoing, "animal", split_axis=0, concat_axis=0, tiled=True)
    incoming = incoming.reshape(-1, share, BLK)
    part_blocks = part_rows // BLK
    shares = []
    for part in range(parts):
        relative = pedigree(own, incoming, rel_index, rel_count, rel_prec, part * part_blocks, part_blocks)
        shares.append([relative] + [turn(relative, devices, shift) for shift in range(1, devices)])

    own_rows = width // groups
    sums = ()
    for part in range(parts):
        kind = jnp.float32 if part < parts - 1 else jnp.bfloat16
        sums = backward_product(genotypes, shares[part], place, 1.0 / math.sqrt(groups * rows), part, kind, sums)
    low, high = [total.reshape(groups, own_rows, half) for total in sums]
    levels = list(range(groups.bit_length() - 1))
    gradient = jnp.concatenate(
        [
            halving_sum(low, groups, levels),
            halving_sum(high, groups, levels[:1] + levels[:0:-1]),
        ],
        axis=1,
    )
    start = lax.axis_index("animal") * own_rows
    own_ridge = lax.dynamic_slice_in_dim(ridge, start, own_rows, 0)
    own_direction = lax.dynamic_slice_in_dim(direction, start, own_rows, 0)
    return gradient + own_ridge[:, None] * own_direction.astype(jnp.float32)


def solution(mesh):
    in_specs = (
        P("animal", "marker"),
        P("marker", None),
        P("marker"),
        P("animal", None, None),
        P("animal", None),
        P("animal"),
        P("animal", None, None, None),
    )
    out_specs = P(("marker", "animal"), None)
    return jax.shard_map(local, mesh=mesh, in_specs=in_specs, out_specs=out_specs, check_vma=False)
```

```python
import functools
import math

import jax
import jax.numpy as jnp
from jax import lax
from jax.experimental import pallas as pl
from jax.experimental.pallas import tpu as pltpu
from jax.sharding import PartitionSpec as P

MARKERS = 25600
BLK = 128
MARK = 16
VMEM_LIMIT = 63 * 1024 * 1024


def divisor(total, unit, most):
    best = unit
    for size in range(unit, most + 1, unit):
        if total % size == 0:
            best = size
    return best


def forward_kernel(scale, devices, place_ref, upper_ref, lower_ref, direction_ref, own_ref, *rest):
    sent, turned = rest[:-1], rest[-1]
    blocks, share, _ = own_ref.shape
    product = scale * jnp.concatenate(
        [
            jnp.dot(geno_ref[...], direction_ref[...], preferred_element_type=jnp.float32)
            for geno_ref in (upper_ref, lower_ref)
        ],
        axis=0,
    )
    largest = jnp.max(jnp.abs(product), axis=(0, 1), keepdims=True)
    power = jnp.clip(jnp.ceil(jnp.log2(largest)), -100.0, 120.0)
    grow = jnp.exp2(14.0 - power)
    turned[...] = product.T
    for shift in range(devices):
        first = pl.multiple_of(lax.rem(place_ref[0] + shift, devices) * share, share)
        for b in range(blocks):
            piece = turned[pl.ds(first, share), b * BLK : (b + 1) * BLK]
            if shift == 0:
                own_ref[b] = piece
            else:
                coded = jnp.round(piece * grow).astype(jnp.int32).astype(jnp.int16)
                sent[shift - 1][b * share : (b + 1) * share] = coded
        if shift > 0:
            mark = jnp.broadcast_to(power, (MARK, BLK)).astype(jnp.int32).astype(jnp.int16)
            sent[shift - 1][blocks * share :] = mark


def forward_product(genotypes, direction, place, devices, scale, first, rows, tile):
    depth, cols = direction.shape
    start = first // tile
    share = cols // devices
    blocks = tile // BLK
    coded = blocks * share + MARK
    steps = rows // tile
    return pl.pallas_call(
        functools.partial(forward_kernel, scale, devices),
        grid_spec=pltpu.PrefetchScalarGridSpec(
            num_scalar_prefetch=1,
            grid=(steps,),
            in_specs=[
                pl.BlockSpec((tile // 2, depth), lambda i, *_: (2 * (start + i), 0)),
                pl.BlockSpec((tile // 2, depth), lambda i, *_: (2 * (start + i) + 1, 0)),
                pl.BlockSpec((depth, cols), lambda i, *_: (0, 0), pipeline_mode=pl.Buffered(1)),
            ],
            out_specs=[pl.BlockSpec((blocks, share, BLK), lambda i, *_: (i, 0, 0))]
            + [pl.BlockSpec((coded, BLK), lambda i, *_: (i, 0))] * (devices - 1),
            scratch_shapes=[pltpu.VMEM((cols, tile), jnp.float32)],
        ),
        out_shape=[jax.ShapeDtypeStruct((steps * blocks, share, BLK), jnp.float32)]
        + [jax.ShapeDtypeStruct((steps * coded, BLK), jnp.int16)] * (devices - 1),
        compiler_params=pltpu.CompilerParams(vmem_limit_bytes=VMEM_LIMIT),
        cost_estimate=pl.CostEstimate(
            flops=2 * rows * depth * cols,
            bytes_accessed=2 * (rows + cols) * depth + 2 * rows * cols,
            transcendentals=0,
        ),
        name="forward_product",
    )(place, genotypes, genotypes, direction)


def settle_kernel(parts, blocks, list_ref, *refs):
    owns, coded, (sum_ref, out_ref) = refs[:parts], refs[parts:-2], refs[-2:]
    share = sum_ref.shape[1]
    size = blocks * share + MARK
    at = 0
    for part, own in enumerate(owns):
        for step in range(own.shape[0] // blocks):
            row = step * size
            total = own[step * blocks : (step + 1) * blocks]
            for ref in coded[part::parts]:
                power = ref[row + blocks * share : row + size].astype(jnp.float32)[:1]
                steps = ref[row : row + blocks * share].astype(jnp.float32)
                total = total + (steps * jnp.exp2(power - 14.0)).reshape(blocks, share, BLK)
            sum_ref[at : at + blocks] = total.astype(sum_ref.dtype)
            at += blocks
    for i in range(out_ref.shape[0]):
        out_ref[i] = sum_ref[list_ref[i]]


def settle(owns, coded, send_list, blocks):
    block_total = sum(own.shape[0] for own in owns)
    share = owns[0].shape[1]
    sends = send_list.size
    flat = [ref for one in coded for ref in one]
    return pl.pallas_call(
        functools.partial(settle_kernel, len(owns), blocks),
        grid_spec=pltpu.PrefetchScalarGridSpec(
            num_scalar_prefetch=1,
            grid=(1,),
            in_specs=[pl.BlockSpec(x.shape, lambda i, *_, n=x.ndim: (0,) * n) for x in (*owns, *flat)],
            out_specs=[
                pl.BlockSpec((block_total, share, BLK), lambda i, *_: (0, 0, 0)),
                pl.BlockSpec((sends, share, BLK), lambda i, *_: (0, 0, 0)),
            ],
        ),
        out_shape=[
            jax.ShapeDtypeStruct((block_total, share, BLK), jnp.bfloat16),
            jax.ShapeDtypeStruct((sends, share, BLK), jnp.bfloat16),
        ],
        compiler_params=pltpu.CompilerParams(vmem_limit_bytes=VMEM_LIMIT),
        name="settle",
    )(send_list.reshape(-1), *owns, *flat)


def pedigree_kernel(group, own_total, start, index_ref, count_ref, own_ref, far_ref, prec_ref, out_ref, table):
    step = pl.program_id(0)

    @pl.when(step == 0)
    def _():
        table[:own_total] = own_ref[...]
        table[own_total:] = far_ref[...]

    for b in range(group):
        block = start + step * group + b
        total = None
        for j in range(prec_ref.shape[1]):
            source = table[index_ref[block, j]]
            source = jnp.where(j < count_ref[block], source, jnp.zeros_like(source))
            term = lax.dot_general(
                prec_ref[b, j], source, (((1,), (1,)), ((), ())), preferred_element_type=jnp.float32
            )
            total = term if total is None else total + term
        out_ref[b] = total.T.astype(out_ref.dtype)


def pedigree(blocked, incoming, rel_index, rel_count, rel_prec, start, count):
    block_total, share, _ = blocked.shape
    far_total = incoming.shape[0]
    slots = rel_prec.shape[1]
    group = divisor(math.gcd(count, start), 1, 6)
    first = start // group
    return pl.pallas_call(
        functools.partial(pedigree_kernel, group, block_total, start),
        grid_spec=pltpu.PrefetchScalarGridSpec(
            num_scalar_prefetch=2,
            grid=(count // group,),
            in_specs=[
                pl.BlockSpec((block_total, share, BLK), lambda i, *_: (0, 0, 0), pipeline_mode=pl.Buffered(1)),
                pl.BlockSpec((far_total, share, BLK), lambda i, *_: (0, 0, 0), pipeline_mode=pl.Buffered(1)),
                pl.BlockSpec((group, slots, BLK, BLK), lambda i, *_: (first + i, 0, 0, 0)),
            ],
            out_specs=pl.BlockSpec((group, share, BLK), lambda i, *_: (i, 0, 0)),
            scratch_shapes=[pltpu.VMEM((block_total + far_total, share, BLK), jnp.bfloat16)],
        ),
        out_shape=jax.ShapeDtypeStruct((count, share, BLK), jnp.bfloat16),
        compiler_params=pltpu.CompilerParams(vmem_limit_bytes=VMEM_LIMIT),
        name="pedigree",
    )(rel_index, rel_count, blocked, incoming, rel_prec)


def backward_kernel(scale, devices, lanes, place_ref, *refs):
    geno, shares, sums = refs[:lanes], refs[lanes : lanes + devices], refs[lanes + devices : -3]
    low_ref, high_ref, effects = refs[-3:]
    half = low_ref.shape[1]
    blocks, share, _ = shares[0].shape

    @pl.when(pl.program_id(0) == 0)
    def _():
        for b in range(blocks):
            pieces = []
            for origin in range(devices):
                piece = shares[0][b]
                for shift in range(1, devices):
                    here = place_ref[0] == (origin + shift) % devices
                    piece = jnp.where(here, shares[shift][b], piece)
                pieces.append(piece)
            effects[b * BLK : (b + 1) * BLK, :] = jnp.concatenate(pieces, axis=0).T

    for lane, geno_ref in enumerate(geno):
        tile = geno_ref.shape[1]
        rows = slice(lane * tile, (lane + 1) * tile)
        product = scale * lax.dot_general(
            geno_ref[...], effects[...], (((0,), (0,)), ((), ())), preferred_element_type=jnp.float32
        )
        low, high = product[:, :half], product[:, half:]
        if sums:
            low, high = low + sums[0][rows, :], high + sums[1][rows, :]
        low_ref[rows, :] = low.astype(low_ref.dtype)
        high_ref[rows, :] = high.astype(high_ref.dtype)


def backward_product(genotypes, shares, place, scale, part, kind, sums=()):
    width = genotypes.shape[1]
    devices = len(shares)
    rows = shares[0].shape[0] * BLK
    cols = devices * shares[0].shape[1]
    lanes = 2 if width % (2 * BLK) == 0 else 1
    tile = divisor(width // lanes, BLK, 5 * BLK)
    half = pl.BlockSpec((lanes * tile, cols // 2), lambda i, *_: (i, 0))
    return pl.pallas_call(
        functools.partial(backward_kernel, scale, devices, lanes),
        grid_spec=pltpu.PrefetchScalarGridSpec(
            num_scalar_prefetch=1,
            grid=(width // (lanes * tile),),
            in_specs=[pl.BlockSpec((rows, tile), lambda i, *_, k=k: (part, lanes * i + k)) for k in range(lanes)]
            + [pl.BlockSpec(s.shape, lambda i, *_: (0, 0, 0), pipeline_mode=pl.Buffered(1)) for s in shares]
            + [half] * len(sums),
            out_specs=[half] * 2,
            scratch_shapes=[pltpu.VMEM((rows, cols), jnp.bfloat16)],
        ),
        out_shape=[jax.ShapeDtypeStruct((width, cols // 2), kind)] * 2,
        compiler_params=pltpu.CompilerParams(vmem_limit_bytes=VMEM_LIMIT),
        cost_estimate=pl.CostEstimate(
            flops=2 * rows * width * cols,
            bytes_accessed=2 * rows * (width + cols) + 4 * width * cols * (2 if sums else 1),
            transcendentals=0,
        ),
        name="backward_product",
    )(place, *[genotypes] * lanes, *shares, *sums)


def turn(value, devices, shift):
    return lax.ppermute(value, "marker", [(d, (d + shift) % devices) for d in range(devices)])


def halving_sum(blocks, devices, bits):
    levels = devices.bit_length() - 1
    here = lax.axis_index("animal")
    terms = [blocks.reshape((2,) * levels + blocks.shape[1:])]
    left = list(range(levels - 1, -1, -1))
    for bit in bits:
        axis = left.index(bit)
        mine = (here >> bit) & 1
        sent, kept = [
            [lax.dynamic_index_in_dim(term, side, axis, keepdims=False) for term in terms]
            for side in (1 - mine, mine)
        ]
        sent = sum(term.astype(jnp.float32) for term in sent).astype(jnp.bfloat16)
        terms = kept + [lax.ppermute(sent, "animal", [(d, d ^ (1 << bit)) for d in range(devices)])]
        left.pop(axis)
    return sum(term.astype(jnp.float32) for term in terms)


def local(genotypes, direction, ridge, send_list, rel_index, rel_count, rel_prec):
    rows, width = genotypes.shape
    half = direction.shape[1] // 2
    groups = lax.axis_size("animal")
    devices = lax.axis_size("marker")
    place = lax.axis_index("marker").reshape(1)
    parts = 2
    part_rows = rows // parts
    tile = divisor(part_rows, BLK, 4 * BLK)

    owns, coded = [], [[] for _ in range(1, devices)]
    for part in range(parts):
        own, *sent = forward_product(
            genotypes, direction, place, devices, 1.0 / math.sqrt(MARKERS), part * part_rows, part_rows, tile
        )
        owns.append(own)
        if part > 0:
            later, earlier = lax.optimization_barrier((sent[1:], [one[-1] for one in coded]))
            sent = [sent[0], *later]
            for one, value in zip(coded, earlier):
                one[-1] = value
        for shift in range(1, devices):
            coded[shift - 1].append(turn(sent[shift - 1], devices, shift))
    own, outgoing = settle(owns, coded, send_list, tile // BLK)

    share = own.shape[1]
    outgoing = outgoing.reshape(groups, -1, share, BLK)
    incoming = lax.all_to_all(outgoing, "animal", split_axis=0, concat_axis=0, tiled=True)
    incoming = incoming.reshape(-1, share, BLK)
    part_blocks = part_rows // BLK
    shares = []
    for part in range(parts):
        relative = pedigree(own, incoming, rel_index, rel_count, rel_prec, part * part_blocks, part_blocks)
        shares.append([relative] + [turn(relative, devices, shift) for shift in range(1, devices)])

    own_rows = width // groups
    sums = ()
    for part in range(parts):
        kind = jnp.float32 if part < parts - 1 else jnp.bfloat16
        sums = backward_product(genotypes, shares[part], place, 1.0 / math.sqrt(groups * rows), part, kind, sums)
    low, high = [total.reshape(groups, own_rows, half) for total in sums]
    levels = list(range(groups.bit_length() - 1))
    gradient = jnp.concatenate(
        [
            halving_sum(low, groups, levels),
            halving_sum(high, groups, levels[:1] + levels[:0:-1]),
        ],
        axis=1,
    )
    start = lax.axis_index("animal") * own_rows
    own_ridge = lax.dynamic_slice_in_dim(ridge, start, own_rows, 0)
    own_direction = lax.dynamic_slice_in_dim(direction, start, own_rows, 0)
    return gradient + own_ridge[:, None] * own_direction.astype(jnp.float32)


def solution(mesh):
    in_specs = (
        P("animal", "marker"),
        P("marker", None),
        P("marker"),
        P("animal", None, None),
        P("animal", None),
        P("animal"),
        P("animal", None, None, None),
    )
    out_specs = P(("marker", "animal"), None)
    return jax.shard_map(local, mesh=mesh, in_specs=in_specs, out_specs=out_specs, check_vma=False)
```
